512 devices in a mesh: dp: 32 (over z_hi, y, core), tensor: 16 (over z_lo, x).
Axes of the slice: x: 4, y: 4, z: 16 (z_hi: 4, z_lo: 4; z = z_hi * 4 + z_lo), core: 2. Of those that a mesh axis runs over, the one named last changes fastest.
Arguments:
- hidden_in: bfloat16 [24576, 4096], P('dp', 'tensor'), may hold values from -40 to 40
- live_rows: int32 [32], replicated, may hold values from 1 to 768, 8192 in all
- sample_tokens: int32 [4], replicated, may hold values from 1 to 4096, 8192 in all
- w_up: bfloat16 [4096, 12288], P('dp', 'tensor'), may hold values from -3 to 3
- w_down: bfloat16 [12288, 4096], P('tensor', 'dp'), may hold values from -0.109375 to 0.109375
- modulation: float32 [3, 4, 4096], P(None, None, 'tensor'), may hold values from -3 to 3
- out_grad: bfloat16 [8192, 4096], P('dp', 'tensor'), may hold values from -6 to 6
Outputs:
- block_out: bfloat16 [8192, 4096], P('dp', 'tensor')
- input_grad: bfloat16 [24576, 4096], P('dp', 'tensor')
- mod_grad: float32 [3, 4, 4096], P(None, None, 'tensor')
The draws below stay inside these ranges and needn't reach their ends.
Inputs may be any that keep to these rules, and one draw needn't show every extreme that they name: `live_rows`: the entries sum to 8192. `sample_tokens`: the entries sum to 8192.
All inputs are finite; a program needn't handle non-finite values.
Results may differ from the reference program's by a relative error of at most 0.023.
Values may be sent and summed in bfloat16 or wider, within the bound.
No kernel may reach another device: no remote copies, remote signals or barrier semaphores. Data moves between devices by JAX's collectives and lax.ppermute only.
A program may use at most 64 MiB of HBM per device.

```python
import math
import jax
import jax.numpy as jnp
import numpy as np
from jax import lax

D = 4096
FF = 12288
SAMPLES = 4
BAL = 256
HID_DEV = 768
IN_CAP = 768
TOTAL = 8192
ROWS_IN = 24576
N_DP = 32
N_TENSOR = 16


def draw_hidden_in(key, part):
    key = jax.random.fold_in(key, 17)
    base_key, column_key, row_key = jax.random.split(key, 3)
    row_power = jax.random.uniform(row_key, (ROWS_IN, 1), jnp.float32, -0.5, 0.5)
    base = jnp.clip(jax.random.normal(base_key, (ROWS_IN, D), jnp.float32), -4.0, 4.0)
    column_power = jax.random.uniform(column_key, (D,), jnp.float32, -0.5, 0.5)
    values = base * jnp.power(10.0, column_power)[None, :] * jnp.power(10.0, row_power)
    return values.astype(jnp.bfloat16)


def draw_w_up(key, part):
    key = jax.random.fold_in(key, 29)
    noise_key, sign_key, pair_key = jax.random.split(key, 3)
    unit = float(D) ** (-0.5)
    noise = jnp.clip(jax.random.normal(noise_key, (D, FF), jnp.float32), -4.0, 4.0)
    pairing = jax.random.permutation(pair_key, N_TENSOR).astype(jnp.int32)
    feature_block = (jnp.arange(D, dtype=jnp.int32) // (D // N_TENSOR)).astype(jnp.int32)
    unit_block = (jnp.arange(FF, dtype=jnp.int32) // (FF // N_TENSOR)).astype(jnp.int32)
    paired = pairing[unit_block][None, :] == feature_block[:, None]
    noise = jnp.where(paired, 3.0 * noise, noise)
    signs = jnp.where(jax.random.uniform(sign_key, (FF,), jnp.float32) < 0.5, -1.0, 1.0)
    values = unit * (noise + 0.5 * signs[None, :])
    return values.astype(jnp.bfloat16)


def raised(array, rng, source, target, blocks, factor):
    owner, partner = [(jnp.arange(array.shape[position]) // (array.shape[position] // blocks)).reshape([-1 if axis == position else 1 for axis in range(array.ndim)]) for position in (source, target)]
    chosen = jax.random.permutation(rng, blocks)[partner]
    strong = (owner == chosen) | (owner == (partner + blocks // 2) % blocks)
    return jnp.where(strong, factor * array, array)


def shard_levels(own_key, extent, cuts, smallest, largest):
    loudness, own = 1.0, jax.random.fold_in(own_key, 6)
    for position, parts in cuts:
        heights = jnp.exp(jax.random.uniform(jax.random.fold_in(own, position), (parts,), jnp.float32, smallest / len(cuts), largest / len(cuts)))
        loudness = loudness * jnp.repeat(heights, extent[position] // parts).reshape([-1 if axis == position else 1 for axis in range(len(extent))])
    return loudness


def profile(number_of, total, most, lean):
    weights = [(1 << 20) // math.isqrt(standing ** lean) + 1 for standing in range(2, number_of + 1)]
    spare, given = total - most - (number_of - 1), [1] * (number_of - 1)
    while spare > 0:
        free = [i for i in range(number_of - 1) if given[i] < most]
        pool, budget = sum([weights[i] for i in free]), spare
        for i in free:
            addition = min(most - given[i], max(1, budget * weights[i] // pool), spare)
            given[i] = given[i] + addition
            spare = spare - addition
    return np.array([most] + given)


def uneven(key, number_of, total, bound, skew):
    if number_of == 2:
        one = jax.random.randint(key, (), max(1, total - bound), min(bound, total - 1) + 1)
        return jnp.stack([one, total - one])
    sizes = jnp.asarray(profile(number_of, total, bound, skew), jnp.int32)
    pairs = (number_of - 1) // 2
    source_of, sink = sizes[1:1 + 2 * pairs:2], sizes[2:2 + 2 * pairs:2]
    slack = jnp.minimum(source_of - 1, bound - sink)
    shifted = jax.random.randint(jax.random.fold_in(key, 1), (pairs,), 0, 1 << 20) % (slack + 1)
    sizes = sizes.at[1:1 + 2 * pairs:2].set(source_of - shifted).at[2:2 + 2 * pairs:2].set(sink + shifted)
    return sizes[jax.random.permutation(jax.random.fold_in(key, 2), number_of)]


def bell_draw(key, shape, deviation, bound, pieces=(), kind=jnp.bfloat16):
    entries = deviation * jax.random.normal(key, shape, jnp.float32)
    if pieces:
        entries = entries * shard_levels(key, shape, pieces, -0.22, 0.18)
    return jnp.clip(entries, -bound, bound).astype(kind)


def heavy_noise(stream_key, dims, deviation, most, shards, heavy, held_as=jnp.bfloat16):
    drawn = deviation * jax.random.normal(stream_key, dims, jnp.float32)
    if shards:
        drawn = drawn * shard_levels(stream_key, dims, shards, -0.22, 0.18)
    return jnp.clip(raised(drawn, jax.random.fold_in(stream_key, 3), *heavy), -most, most).astype(held_as)


def setup_inputs(seed: int = 0) -> dict:
    streams_of = jax.random.split(jax.random.key(seed), 8)
    return {
        "hidden_in": draw_hidden_in(jax.random.fold_in(streams_of[7], 71), 0),
        "live_rows": uneven(streams_of[1], N_DP, TOTAL, IN_CAP, 2).astype(jnp.int32),
        "sample_tokens": uneven(streams_of[2], SAMPLES, TOTAL, TOTAL // 2, 1).astype(jnp.int32),
        "w_up": draw_w_up(jax.random.fold_in(streams_of[7], 71), 0),
        "w_down": heavy_noise(streams_of[4], (FF, D), FF ** -0.5, 0.109375, ((0, 16), (1, 32)), (0, 1, 32, 2.75)),
        "modulation": bell_draw(streams_of[5], (3, SAMPLES, D), 0.6, 3.0, ((2, 16),), jnp.float32),
        "out_grad": bell_draw(streams_of[6], (TOTAL, D), 1.0, 6.0, ((0, 32), (1, 16))),
    }


GELU_K = 0.7978845608028654
GELU_C = 0.044715
EPS = 1e-06

def gelu_value(pre):
    inner = GELU_K * (pre + GELU_C * pre * pre * pre)
    return 0.5 * pre * (1.0 + jnp.tanh(inner))

def gelu_slope(pre):
    inner = GELU_K * (pre + GELU_C * pre * pre * pre)
    tangent = jnp.tanh(inner)
    return 0.5 * (1.0 + tangent) + 0.5 * pre * (1.0 - tangent * tangent) * GELU_K * (1.0 + 3.0 * GELU_C * pre * pre)

def contract_last(left, right):
    return lax.dot_general(left, right, (((1,), (1,)), ((), ())), preferred_element_type=jnp.float32)

def reference(hidden_in, live_rows, sample_tokens, w_up, w_down, modulation, out_grad):
    row_ends = jnp.cumsum(live_rows).astype(jnp.int32)
    row_starts = (row_ends - live_rows).astype(jnp.int32)
    device_ids = jnp.arange(N_DP, dtype=jnp.int32)[:, None]
    slot_ids = jnp.arange(BAL, dtype=jnp.int32)[None, :]
    global_rows = (device_ids + N_DP * slot_ids).reshape(-1).astype(jnp.int32)
    owners = lax.optimization_barrier(jnp.sum((row_ends[None, :] <= global_rows[:, None]).astype(jnp.int32), axis=1)).astype(jnp.int32)
    source_rows = (owners * IN_CAP + global_rows - row_starts[owners]).astype(jnp.int32)
    rows_f = hidden_in[source_rows].astype(jnp.float32)
    sample_ends = jnp.cumsum(sample_tokens).astype(jnp.int32)
    sample_starts = (sample_ends - sample_tokens).astype(jnp.int32)
    member = ((global_rows[:, None] >= sample_starts[None, :]) & (global_rows[:, None] < sample_ends[None, :])).astype(jnp.float32)
    shift_rows = jnp.dot(member, modulation[0], precision=lax.Precision.HIGHEST)
    scale_rows = jnp.dot(member, modulation[1], precision=lax.Precision.HIGHEST)
    gate_rows = jnp.dot(member, modulation[2], precision=lax.Precision.HIGHEST)
    average = lax.optimization_barrier(jnp.mean(rows_f, axis=1, keepdims=True))
    centred = rows_f - average
    spread = lax.optimization_barrier(jnp.mean(centred * centred, axis=1, keepdims=True))
    inv_scale = lax.rsqrt(spread + EPS)
    normed = centred * inv_scale
    modulated = (normed * (1.0 + scale_rows) + shift_rows).astype(jnp.bfloat16)
    grad_f = out_grad.astype(jnp.float32)
    scaled_grad = (gate_rows * grad_f).astype(jnp.bfloat16)

    def block_step(carry, index):
        start = (index * HID_DEV).astype(jnp.int32)
        up_block = lax.dynamic_slice_in_dim(w_up, start, HID_DEV, 1)
        down_block = lax.dynamic_slice_in_dim(w_down, start, HID_DEV, 0)
        pre = jnp.dot(modulated, up_block, preferred_element_type=jnp.float32)
        hidden = gelu_value(pre).astype(jnp.bfloat16)
        out_part = jnp.dot(hidden, down_block, preferred_element_type=jnp.float32).astype(jnp.bfloat16)
        hidden_grad = contract_last(scaled_grad, down_block)
        pre_grad = (hidden_grad * gelu_slope(pre)).astype(jnp.bfloat16)
        in_part = contract_last(pre_grad, up_block).astype(jnp.bfloat16)
        return ((carry[0] + out_part.astype(jnp.float32), carry[1] + in_part.astype(jnp.float32)), None)
    zeros_block = jnp.zeros((TOTAL, D), jnp.float32)
    totals, unused = lax.scan(block_step, (zeros_block, zeros_block), jnp.arange(FF // HID_DEV, dtype=jnp.int32))
    branch, mod_in_grad = totals
    block_out = (rows_f + gate_rows * branch).astype(jnp.bfloat16)
    normed_grad = mod_in_grad * (1.0 + scale_rows)
    first_mean = lax.optimization_barrier(jnp.mean(normed_grad, axis=1, keepdims=True))
    second_mean = lax.optimization_barrier(jnp.mean(normed_grad * normed, axis=1, keepdims=True))
    row_grad = (grad_f + inv_scale * (normed_grad - first_mean - normed * second_mean)).astype(jnp.bfloat16)
    input_grad = jnp.zeros((ROWS_IN, D), jnp.bfloat16).at[source_rows].set(row_grad)

    def sample_totals(values):
        return lax.dot_general(member, values, (((0,), (0,)), ((), ())), precision=lax.Precision.HIGHEST)
    mod_grad = jnp.stack([sample_totals(mod_in_grad), sample_totals(mod_in_grad * normed), sample_totals(grad_f * branch)])
    return (block_out, input_grad, mod_grad)
```

```python
import jax
import jax.numpy as jnp
from jax import lax
from jax.experimental import pallas as pl
from jax.experimental.pallas import tpu as pltpu
from jax.sharding import Mesh, PartitionSpec as P

GELU_K = 0.7978845608028654
GELU_C = 0.044715
EPS = 1e-06
AXES = ("zh", "y", "c", "zl", "x")
SIZES = (4, 4, 2, 4, 4)
DP = ("zh", "y", "c")
TP = ("zl", "x")
SAMPLES = 4
VMEM = 48 * 1024 * 1024


def gelu_value(pre):
    inner = GELU_K * (pre + GELU_C * pre * pre * pre)
    return 0.5 * pre * (1.0 + jnp.tanh(inner))


def gelu_slope(pre):
    inner = GELU_K * (pre + GELU_C * pre * pre * pre)
    tangent = jnp.tanh(inner)
    return 0.5 * (1.0 + tangent) + 0.5 * pre * (1.0 - tangent * tangent) * GELU_K * (
        1.0 + 3.0 * GELU_C * pre * pre
    )


def contract_last(left, right):
    return lax.dot_general(
        left, right, (((1,), (1,)), ((), ())), preferred_element_type=jnp.float32
    )


def sample_totals(member, values):
    return lax.dot_general(
        member, values, (((0,), (0,)), ((), ())), precision=lax.Precision.HIGHEST
    )


def shifted(value, axis, step):
    size = lax.axis_size(axis)
    return lax.ppermute(value, axis, [(i, (i + step) % size) for i in range(size)])


def crossed(value, axis, mask):
    size = lax.axis_size(axis)
    return lax.ppermute(value, axis, [(i, i ^ mask) for i in range(size)])


def ring_pieces(value, axis):
    half = value.shape[0] // 2
    before = shifted(value, axis, 1)
    after = shifted(value, axis, -1)
    far = jnp.concatenate(
        [shifted(before[:half], axis, 1), shifted(after[half:], axis, -1)], axis=0
    )
    return value, before, far, after


def spread(value, axis):
    copies = jnp.broadcast_to(value[None], (lax.axis_size(axis),) + value.shape)
    return lax.all_to_all(copies, axis, split_axis=0, concat_axis=0, tiled=True)


def summed(value, axis):
    if lax.axis_size(axis) == 2:
        return value + crossed(value, axis, 1)
    return (value + crossed(value, axis, 1)) + (crossed(value, axis, 2) + crossed(value, axis, 3))


def gathered_weight(part):
    over_zh = jnp.stack(ring_pieces(part, "zh"))
    own = ring_pieces(over_zh, "y")
    other = tuple(shifted(piece, "c", 1) for piece in own)
    return own + other


def sample_mix(member, table):
    out = jnp.broadcast_to(table[SAMPLES - 1 : SAMPLES], (member.shape[0], table.shape[1]))
    for q in range(SAMPLES - 1):
        out = jnp.where(member[:, q : q + 1] > 0.5, table[q : q + 1], out)
    return out


def prepare_kernel(place, rows, grad, modulation, member, mod_out, grad_out, average, inv_scale):
    y, zh, c = place[0], place[1], place[2]
    live = member[...]
    count = rows.shape[0]
    width = rows.shape[3]
    half = width // 2
    features = count * count * width

    total = jnp.zeros(rows.shape[2:], jnp.float32)
    for i in range(count):
        for j in range(count):
            total = total + rows[i, j].astype(jnp.float32)
    mean = jnp.sum(total, axis=1, keepdims=True) / features
    total = jnp.zeros(rows.shape[2:], jnp.float32)
    for i in range(count):
        for j in range(count):
            centred = rows[i, j].astype(jnp.float32) - mean
            total = total + centred * centred
    inv = lax.rsqrt(jnp.sum(total, axis=1, keepdims=True) / features + EPS)
    average[...] = mean
    inv_scale[...] = inv

    def step(index, carry):
        dy, dz = index // count, index % count
        xi = lax.rem(y - dy + count, count)
        zi = lax.rem(zh - dz + count, count)
        table = modulation[zi * count + xi]
        shift, scale, gate = table[0:4], table[4:8], table[8:12]
        normed = (rows[xi, zi].astype(jnp.float32) - mean) * inv
        value = (normed * (1.0 + sample_mix(live, scale)) + sample_mix(live, shift)).astype(
            jnp.bfloat16
        )
        gated = (sample_mix(live, gate) * grad[xi, zi].astype(jnp.float32)).astype(jnp.bfloat16)
        first = pl.ds(pl.multiple_of(c * half, half), half)
        second = pl.ds(pl.multiple_of((1 - c) * half, half), half)
        mod_out[dy, dz, :, first] = value[:, :half]
        mod_out[dy, dz, :, second] = value[:, half:]
        grad_out[dy, dz, :, first] = gated[:, :half]
        grad_out[dy, dz, :, second] = gated[:, half:]
        return carry

    lax.fori_loop(0, count * count, step, 0)


def product_in(blocks, pieces, total):
    count = blocks.shape[0]
    total[...] = jnp.zeros_like(total)
    for dy in range(count):
        own, other = pieces[dy], pieces[count + dy]

        def step(dz, carry, dy=dy, own=own, other=other):
            weight = jnp.concatenate([own[dz], other[dz]], axis=0)
            total[...] += jnp.dot(blocks[dy, dz], weight, preferred_element_type=jnp.float32)
            return carry

        lax.fori_loop(0, count, step, 0)


def product_out(place, hidden, pieces, out):
    y, zh, c = place[0], place[1], place[2]
    count = out.shape[0]
    half = out.shape[3] // 2
    first = pl.ds(pl.multiple_of(c * half, half), half)
    second = pl.ds(pl.multiple_of((1 - c) * half, half), half)
    for dy in range(count):
        own, other = pieces[dy], pieces[count + dy]

        def step(dz, carry, dy=dy, own=own, other=other):
            weight = jnp.concatenate([own[dz], other[dz]], axis=0)
            value = contract_last(hidden[...], weight).astype(jnp.bfloat16)
            xi = lax.rem(y - dy + count, count)
            zi = lax.rem(zh - dz + count, count)
            out[xi, zi, :, first] = value[:, :half]
            out[xi, zi, :, second] = value[:, half:]
            return carry

        lax.fori_loop(0, count, step, 0)


def forward_kernel(place, blocks, *refs):
    up, down = refs[:8], refs[8:16]
    pre, out, hidden = refs[16:]
    product_in(blocks, up, pre)
    hidden[...] = gelu_value(pre[...]).astype(jnp.bfloat16)
    product_out(place, hidden, down, out)


def backward_kernel(place, blocks, pre, *refs):
    up, down = refs[:8], refs[8:16]
    out, total, pre_grad = refs[16:]
    product_in(blocks, down, total)
    pre_grad[...] = (total[...] * gelu_slope(pre[...])).astype(jnp.bfloat16)
    product_out(place, pre_grad, up, out)


SMEM_SPEC = pl.BlockSpec(memory_space=pltpu.SMEM)
VMEM_SPEC = pl.BlockSpec(memory_space=pltpu.VMEM)


def call(kernel, outs, scratch, flops, moved, *args):
    return pl.pallas_call(
        kernel,
        out_shape=outs,
        in_specs=[SMEM_SPEC] + [VMEM_SPEC] * (len(args) - 1),
        out_specs=jax.tree.map(lambda _: VMEM_SPEC, outs),
        scratch_shapes=scratch,
        compiler_params=pltpu.CompilerParams(vmem_limit_bytes=VMEM),
        cost_estimate=pl.CostEstimate(flops=flops, bytes_accessed=moved, transcendentals=0),
    )(*args)


def scattered_sum(blocks):
    from_x = lax.all_to_all(blocks, "x", split_axis=0, concat_axis=0, tiled=True)
    over_x = jnp.sum(from_x.astype(jnp.float32), axis=0).astype(jnp.bfloat16)
    from_zl = lax.all_to_all(over_x, "zl", split_axis=0, concat_axis=0, tiled=True)
    return jnp.sum(from_zl.astype(jnp.float32), axis=0)


def body(hidden_in, live_rows, sample_tokens, w_up, w_down, modulation, out_grad):
    groups = lax.axis_size(DP)
    position = lax.axis_index(DP)
    slots_in = hidden_in.shape[0]
    per_pair = slots_in // groups
    balanced = out_grad.shape[0]
    width_local = hidden_in.shape[1]
    tensor_count = lax.axis_size(TP)
    model_width = width_local * tensor_count
    hid = w_up.shape[1]
    f32, bf16 = jnp.float32, jnp.bfloat16
    shape = jax.ShapeDtypeStruct

    up = gathered_weight(w_up)
    down = gathered_weight(w_down.T)

    row_ends = jnp.cumsum(live_rows)
    row_starts = row_ends - live_rows
    device_ids = jnp.arange(groups, dtype=jnp.int32)
    own_start = jnp.sum(jnp.where(device_ids == position, row_starts, 0))
    own_live = jnp.sum(jnp.where(device_ids == position, live_rows, 0))
    slot_ids = jnp.arange(per_pair, dtype=jnp.int32)[None, :]
    first_row = jnp.mod(device_ids[:, None] - own_start, groups)
    local_rows = first_row + groups * slot_ids
    picked = jnp.take(hidden_in, jnp.minimum(local_rows, slots_in - 1).reshape(-1), axis=0)
    outgoing = jnp.where((local_rows < own_live).reshape(-1, 1), picked, jnp.zeros_like(picked))
    outgoing = outgoing.reshape(groups, per_pair, width_local)
    incoming = lax.all_to_all(outgoing, DP, split_axis=0, concat_axis=0, tiled=True)
    global_rows = position + groups * jnp.arange(balanced, dtype=jnp.int32)
    owner_table = (row_ends[None, :] <= global_rows[:, None]).astype(jnp.int32)
    owners = jnp.sum(owner_table, axis=1)
    owner_start = jnp.sum(
        jnp.where(owners[:, None] == device_ids[None, :], row_starts[None, :], 0), axis=1
    )
    owner_slot = (global_rows - owner_start) // groups
    rows_bal = jnp.take(
        incoming.reshape(groups * per_pair, width_local), owners * per_pair + owner_slot, axis=0
    )
    sample_ends = jnp.cumsum(sample_tokens)
    sample_starts = sample_ends - sample_tokens
    member = (
        (global_rows[:, None] >= sample_starts[None, :])
        & (global_rows[:, None] < sample_ends[None, :])
    ).astype(f32)

    rows_all = spread(spread(rows_bal, "zl"), "x")
    grad_all = spread(spread(out_grad, "zl"), "x")
    modulation_all = lax.all_gather(modulation.reshape(-1, width_local), TP, axis=0)

    place = jnp.stack([lax.axis_index("y"), lax.axis_index("zh"), lax.axis_index("c")]).astype(
        jnp.int32
    )
    block_shape = shape(rows_all.shape, bf16)
    column = shape((balanced, 1), f32)
    modulated, scaled_grad, average, inv_scale = call(
        prepare_kernel,
        (block_shape, block_shape, column, column),
        [],
        40 * balanced * model_width,
        8 * balanced * model_width,
        place, rows_all, grad_all, modulation_all, member,
    )
    product = 4 * balanced * model_width * hid
    moved = 4 * model_width * hid
    pre, partial_out = call(
        forward_kernel,
        (shape((balanced, hid), f32), block_shape),
        [pltpu.VMEM((balanced, hid), bf16)],
        product, moved,
        place, modulated, *up, *down,
    )
    (partial_in,) = call(
        backward_kernel,
        (block_shape,),
        [pltpu.VMEM((balanced, hid), f32), pltpu.VMEM((balanced, hid), bf16)],
        product, moved,
        place, scaled_grad, pre, *up, *down,
    )
    branch = scattered_sum(partial_out)
    mod_in_grad = scattered_sum(partial_in)

    shift_scale_gate = [
        jnp.dot(member, modulation[i], precision=lax.Precision.HIGHEST) for i in (1, 2)
    ]
    scale_rows, gate_rows = shift_scale_gate
    rows_f = rows_bal.astype(f32)
    normed = (rows_f - average) * inv_scale
    block_out = (rows_f + gate_rows * branch).astype(bf16)
    grad_f = out_grad.astype(f32)
    normed_grad = mod_in_grad * (1.0 + scale_rows)
    sums = jnp.stack([jnp.sum(normed_grad, axis=1), jnp.sum(normed_grad * normed, axis=1)])
    means = jnp.sum(spread(sums, TP), axis=0) / model_width
    row_grad = (
        grad_f + inv_scale * (normed_grad - means[0][:, None] - normed * means[1][:, None])
    ).astype(bf16)
    local_mod = jnp.stack(
        [
            sample_totals(member, mod_in_grad),
            sample_totals(member, mod_in_grad * normed),
            sample_totals(member, grad_f * branch),
        ]
    )
    mod_grad = summed(summed(summed(local_mod, "c"), "y"), "zh")

    source_first = jnp.mod(position - row_starts[:, None], groups)
    source_rows = source_first + groups * slot_ids
    back_valid = source_rows < live_rows[:, None]
    back_index = (row_starts[:, None] + source_rows - position) // groups
    taken = jnp.take(row_grad, jnp.clip(back_index, 0, balanced - 1).reshape(-1), axis=0)
    returning = jnp.where(back_valid.reshape(-1, 1), taken, jnp.zeros_like(taken)).reshape(
        groups, per_pair, width_local
    )
    arrived = lax.all_to_all(returning, DP, split_axis=0, concat_axis=0, tiled=True)
    own_rows = jnp.arange(slots_in, dtype=jnp.int32)
    target_of = jnp.mod(own_start + own_rows, groups)
    target_slot = own_rows // groups
    gathered_back = jnp.take(
        arrived.reshape(groups * per_pair, width_local), target_of * per_pair + target_slot, axis=0
    )
    input_grad = jnp.where(
        (own_rows < own_live)[:, None], gathered_back, jnp.zeros_like(gathered_back)
    )
    return (block_out, input_grad, mod_grad)


def solution(mesh):
    cut = Mesh(mesh.devices.reshape(SIZES), AXES)
    return jax.shard_map(
        body,
        mesh=cut,
        in_specs=(
            P(DP, TP),
            P(),
            P(),
            P(DP, TP),
            P(TP, DP),
            P(None, None, TP),
            P(DP, TP),
        ),
        out_specs=(P(DP, TP), P(DP, TP), P(None, None, TP)),
        check_vma=False,
    )
```

```python
import functools

import jax
import jax.numpy as jnp
from jax import lax
from jax.experimental import pallas as pl
from jax.experimental.pallas import tpu as pltpu
from jax.sharding import Mesh, PartitionSpec as P

GELU_K = 0.7978845608028654
GELU_C = 0.044715
EPS = 1e-06
AXES = ("zh", "y", "c", "zl", "x")
SIZES = (4, 4, 2, 4, 4)
DP = ("zh", "y", "c")
TP = ("zl", "x")
SAMPLES = 4
VMEM = 48 * 1024 * 1024
US = 10**9


def gelu_value(pre):
    inner = GELU_K * (pre + GELU_C * pre * pre * pre)
    return 0.5 * pre * (1.0 + jnp.tanh(inner))


def gelu_slope(pre):
    inner = GELU_K * (pre + GELU_C * pre * pre * pre)
    tangent = jnp.tanh(inner)
    return 0.5 * (1.0 + tangent) + 0.5 * pre * (1.0 - tangent * tangent) * GELU_K * (
        1.0 + 3.0 * GELU_C * pre * pre
    )


def shifted(value, axis, step):
    size = lax.axis_size(axis)
    return lax.ppermute(value, axis, [(i, (i + step) % size) for i in range(size)])


def crossed(value, axis, mask):
    size = lax.axis_size(axis)
    return lax.ppermute(value, axis, [(i, i ^ mask) for i in range(size)])


def direct_pieces(value, axis):
    return jnp.stack([value] + [shifted(value, axis, k) for k in (1, 2, 3)])


def spread(value, axis):
    copies = jnp.broadcast_to(value[None], (lax.axis_size(axis),) + value.shape)
    return lax.all_to_all(copies, axis, split_axis=0, concat_axis=0, tiled=True)


def summed(value, axis):
    mask = 1
    while mask < lax.axis_size(axis):
        value = value + crossed(value, axis, mask)
        mask *= 2
    return value


def three_terms(value):
    terms = []
    for _ in range(3):
        term = lax.reduce_precision(value, 8, 7)
        terms.append(term.astype(jnp.bfloat16))
        value = value - term
    return terms


def sample_mix(member, table):
    out = jnp.broadcast_to(table[SAMPLES - 1 : SAMPLES], (member.shape[0], table.shape[1]))
    for q in range(SAMPLES - 1):
        out = jnp.where(member[:, q : q + 1] > 0.5, table[q : q + 1], out)
    return out


def halves(c, half):
    first = pl.ds(pl.multiple_of(c * half, half), half)
    second = pl.ds(pl.multiple_of((1 - c) * half, half), half)
    return first, second


def zh_of(zh, n, count):
    step = jnp.where(n == 1, count - 1, jnp.where(n == 2, 1, jnp.where(n == 3, 2, 0)))
    return lax.rem(zh + step, count)


def weight_of(first, first_other, last, last_other, n, which):
    own, other = (first, first_other) if n < 3 else (last, last_other)
    return jnp.concatenate([own[0, n % 3, which], other[0, n % 3, which]], axis=0)


def gate_kernel(place, gathered, member, grad_out, table_out):
    y, zh, c = place[0], place[1], place[2]
    live = member[...]
    count = grad_out.shape[0]
    rows = grad_out.shape[2]
    half = grad_out.shape[3] // 2

    def step(index, carry):
        dy, n = index // count, index % count
        xi = lax.rem(y - dy + count, count)
        zi = zh_of(zh, n, count)
        block = zi * count + xi
        terms = gathered[block, rows : rows + 48].astype(jnp.float32)
        table = (terms[0:16] + terms[16:32]) + terms[32:48]
        table_out[block] = table
        grad = gathered[block, 0:rows].astype(jnp.float32)
        gated = (sample_mix(live, table[8:12]) * grad).astype(jnp.bfloat16)
        first, second = halves(c, half)
        grad_out[dy, n, :, first] = gated[:, :half]
        grad_out[dy, n, :, second] = gated[:, half:]
        return carry

    lax.fori_loop(0, count * count, step, 0)


def rows_kernel(place, rows, table_in, member, mod_out, average, inv_scale):
    y, zh, c = place[0], place[1], place[2]
    live = member[...]
    count = rows.shape[0]
    balanced = rows.shape[2]
    width = rows.shape[3]
    half = width // 2
    features = count * count * width

    total = jnp.zeros(rows.shape[2:], jnp.float32)
    for i in range(count):
        for j in range(count):
            total = total + rows[i, j].astype(jnp.float32)
    mean = jnp.sum(total, axis=1, keepdims=True) / features
    total = jnp.zeros(rows.shape[2:], jnp.float32)
    for i in range(count):
        for j in range(count):
            centred = rows[i, j].astype(jnp.float32) - mean
            total = total + centred * centred
    inv = lax.rsqrt(jnp.sum(total, axis=1, keepdims=True) / features + EPS)
    average[...] = mean
    inv_scale[...] = inv

    def step(index, carry):
        dy, n = index // count, index % count
        xi = lax.rem(y - dy + count, count)
        zi = zh_of(zh, n, count)
        table = table_in[zi * count + xi]
        shift, scale = table[0:4], 1.0 + table[4:8]
        normed = (rows[xi, zi].astype(jnp.float32) - mean) * inv
        value = (normed * sample_mix(live, scale) + sample_mix(live, shift)).astype(jnp.bfloat16)
        scale_hi = scale.astype(jnp.bfloat16).astype(jnp.float32)
        shift_hi = shift.astype(jnp.bfloat16).astype(jnp.float32)
        extra = jnp.concatenate(
            [scale_hi, scale - scale_hi, shift_hi, shift - shift_hi], axis=0
        ).astype(jnp.bfloat16)
        first, second = halves(c, half)
        mod_out[dy, n, 0:balanced, first] = value[:, :half]
        mod_out[dy, n, 0:balanced, second] = value[:, half:]
        mod_out[dy, n, balanced : balanced + 16, first] = extra[:, :half]
        mod_out[dy, n, balanced : balanced + 16, second] = extra[:, half:]
        return carry

    lax.fori_loop(0, count * count, step, 0)


def hidden_kernel(
    modulated, scaled, member, first, first_other, last, last_other,
    hidden_out, pre_grad_out, sums_out, pre_total, grad_total,
):
    live = member[...]
    rows = scaled.shape[2]
    step = pl.program_id(0)

    @pl.when(step == 0)
    def _():
        pre_total[...] = jnp.zeros_like(pre_total)
        grad_total[...] = jnp.zeros_like(grad_total)

    for n in range(scaled.shape[1]):
        up = weight_of(first, first_other, last, last_other, n, 0)
        pre_total[...] += jnp.dot(modulated[0, n], up, preferred_element_type=jnp.float32)
        down = weight_of(first, first_other, last, last_other, n, 1)
        grad_total[...] += jnp.dot(scaled[0, n], down, preferred_element_type=jnp.float32)

    @pl.when(step == pl.num_programs(0) - 1)
    def _():
        pre = pre_total[0:rows]
        extra = pre_total[rows : rows + 16]
        hidden_out[...] = gelu_value(pre).astype(jnp.bfloat16).T
        pre_grad = (grad_total[...] * gelu_slope(pre)).astype(jnp.bfloat16)
        pre_grad_out[...] = pre_grad.T
        pre_grad = pre_grad.astype(jnp.float32)
        scale_part = sample_mix(live, extra[0:4] + extra[4:8])
        shift_part = sample_mix(live, extra[8:12] + extra[12:16])
        first = jnp.sum(pre_grad * scale_part, axis=1, keepdims=True)
        second = jnp.sum(pre_grad * (pre - shift_part), axis=1, keepdims=True)
        lane = lax.broadcasted_iota(jnp.int32, (rows, 128), 1)
        both = jnp.where(lane == 0, first, jnp.where(lane == 1, second, 0.0))
        sums = both.T[0:8]
        high = sums.astype(jnp.bfloat16).astype(jnp.float32)
        sums_out[...] = jnp.concatenate([high, sums - high], axis=0).astype(jnp.bfloat16)


def outward_kernel(place, hidden, first, first_other, last, last_other, *refs):
    out = refs[-1]
    zh, c = place[1], place[2]
    count = out.shape[1]
    rows = out.shape[3]
    half = rows // 2
    low, high = halves(c, half)
    for n in range(count):
        weight = weight_of(first, first_other, last, last_other, n, 0)
        value = jnp.dot(weight, hidden[...], preferred_element_type=jnp.float32).astype(
            jnp.bfloat16
        )
        zi = zh_of(zh, n, count)
        out[0, zi, low, :] = value[:half]
        out[0, zi, high, :] = value[half:]
        if len(refs) == 2:
            out[0, zi, rows : rows + 16, :] = refs[0][...]


def joined_sums(terms):
    total = terms[0:8] + terms[8:16]
    high = total.astype(jnp.bfloat16).astype(jnp.float32)
    return jnp.concatenate([high, total - high], axis=0)


def fold_kernel(place, blocks, *refs):
    zl = place[3]
    count, places, height, width = blocks.shape
    out = refs[0] if height > width else refs[2]

    def step(m, carry):
        total = blocks[0, m].astype(jnp.float32)
        for k in range(1, count):
            total = total + blocks[k, m].astype(jnp.float32)
        to = lax.rem(m - zl + places, places)
        out[to, 0:width] = total[0:width].astype(jnp.bfloat16)
        if height > width:
            out[to, width:height] = joined_sums(total[width:height]).astype(jnp.bfloat16)
        else:
            grad, member, _, totals = refs
            part = image_sums(member[...], grad[m].astype(jnp.float32) * total.T)
            totals[to] = jnp.concatenate(part, axis=0)
        return carry

    lax.fori_loop(0, places, step, 0)


def picked(index, values):
    lanes = lax.broadcasted_iota(jnp.int32, (index.shape[0], values.shape[0]), 1)
    chosen = jnp.where(lanes == index, 1.0, 0.0).astype(jnp.bfloat16)
    return jnp.dot(chosen, values, preferred_element_type=jnp.float32).astype(jnp.bfloat16)


def image_sums(live, values):
    return [
        jnp.sum(jnp.where(live[:, q : q + 1] > 0.5, values, 0.0), axis=0, keepdims=True)
        for q in range(SAMPLES)
    ]


def finish_in_kernel(
    features, piece0, piece1, piece2, piece3,
    rows, grad, average, inv_scale, member, table, index, back, totals,
):
    live = member[...]
    balanced = rows.shape[0]
    total = piece0[...].astype(jnp.float32)
    for piece in (piece1, piece2, piece3):
        total = total + piece[...].astype(jnp.float32)
    mod_in_grad = total[0:balanced].T
    sums = total[balanced : balanced + 8] + total[balanced + 8 : balanced + 16]
    means = jnp.concatenate([sums, jnp.zeros((120, balanced), jnp.float32)], axis=0).T / features
    inv = inv_scale[...]
    normed = (rows[...].astype(jnp.float32) - average[...]) * inv
    normed_grad = mod_in_grad * (1.0 + sample_mix(live, table[4:8]))
    row_grad = grad[...].astype(jnp.float32) + inv * (
        normed_grad - means[:, 0:1] - normed * means[:, 1:2]
    )
    back[...] = picked(index[...], row_grad.astype(jnp.bfloat16))
    totals[...] = jnp.concatenate(
        image_sums(live, mod_in_grad) + image_sums(live, mod_in_grad * normed), axis=0
    )


def finish_out_kernel(piece0, piece1, piece2, piece3, rows, member, table, out):
    live = member[...]
    branch = piece0[...].astype(jnp.float32)
    for piece in (piece1, piece2, piece3):
        branch = branch + piece[...].astype(jnp.float32)
    branch = branch.T
    gate = sample_mix(live, table[8:12])
    out[...] = (rows[...].astype(jnp.float32) + gate * branch).astype(jnp.bfloat16)


def pick_kernel(index, values, out):
    out[...] = picked(index[...], values[...])


SMEM_SPEC = pl.BlockSpec(memory_space=pltpu.SMEM)
VMEM_SPEC = pl.BlockSpec(memory_space=pltpu.VMEM)


def call(kernel, outs, scratch, flops, moved, *args):
    return pl.pallas_call(
        kernel,
        out_shape=outs,
        in_specs=[SMEM_SPEC if a.ndim == 1 else VMEM_SPEC for a in args],
        out_specs=jax.tree.map(lambda _: VMEM_SPEC, outs),
        scratch_shapes=scratch,
        compiler_params=pltpu.CompilerParams(vmem_limit_bytes=VMEM),
        cost_estimate=pl.CostEstimate(flops=flops, bytes_accessed=moved, transcendentals=0),
    )(*args)


def body(hidden_in, live_rows, sample_tokens, w_up, w_down, modulation, out_grad):
    groups = lax.axis_size(DP)
    position = lax.axis_index(DP)
    slots_in = hidden_in.shape[0]
    per_pair = slots_in // groups
    balanced = out_grad.shape[0]
    width_local = hidden_in.shape[1]
    tensor_count = lax.axis_size(TP)
    model_width = width_local * tensor_count
    hid = w_up.shape[1]
    f32, bf16 = jnp.float32, jnp.bfloat16
    shape = jax.ShapeDtypeStruct
    low = groups - 1
    bits = groups.bit_length() - 1

    weights = jnp.stack([w_up, w_down.T])
    before = shifted(weights, "zh", 1)
    after = shifted(weights, "zh", -1)

    table = modulation.reshape(-1, width_local)
    pad = jnp.zeros((16 - table.shape[0], width_local), f32)
    payload = jnp.concatenate([out_grad] + three_terms(jnp.concatenate([table, pad])), axis=0)

    row_ends = jnp.cumsum(live_rows)
    row_starts = row_ends - live_rows
    device_ids = jnp.arange(groups, dtype=jnp.int32)
    own_start = jnp.sum(jnp.where(device_ids < position, live_rows, 0))
    own_live = jnp.sum(jnp.where(device_ids == position, live_rows, 0))
    slot_ids = jnp.arange(per_pair, dtype=jnp.int32)[None, :]
    local_rows = ((device_ids[:, None] - own_start) & low) + groups * slot_ids
    outgoing = hidden_in[local_rows.reshape(-1)].reshape(groups, per_pair, width_local)
    gathered = lax.all_gather(payload, TP, axis=0)
    far = jnp.concatenate([shifted(before[:1], "zh", 1), shifted(after[1:], "zh", -1)], axis=0)
    first = direct_pieces(jnp.stack([weights, before, after]), "y")
    incoming = lax.all_to_all(outgoing, DP, split_axis=0, concat_axis=0, tiled=True)
    global_rows = position + groups * jnp.arange(balanced, dtype=jnp.int32)
    before_row = row_ends[None, :] <= global_rows[:, None]
    owners = jnp.sum(before_row.astype(jnp.int32), axis=1)
    owner_start = jnp.sum(jnp.where(before_row, live_rows[None, :], 0), axis=1)
    owner_slot = (global_rows - owner_start) >> bits
    incoming, far, first = lax.optimization_barrier((incoming, far, first))
    rows_bal = incoming.reshape(groups * per_pair, width_local)[owners * per_pair + owner_slot]
    sample_ends = jnp.cumsum(sample_tokens)
    sample_starts = sample_ends - sample_tokens
    member = (
        (global_rows[:, None] >= sample_starts[None, :])
        & (global_rows[:, None] < sample_ends[None, :])
    ).astype(f32)

    rows_zl = spread(rows_bal, "zl")
    rows_zl, gathered = lax.optimization_barrier((rows_zl, gathered))
    last = direct_pieces(far[None], "y")
    first_other = shifted(first, "c", 1)
    rows_all = spread(rows_zl, "x")

    by_place = gathered.reshape(4, 4, -1, width_local)
    grad_zl = lax.dynamic_index_in_dim(by_place, lax.axis_index("x"), 1, keepdims=False)[:, :balanced]
    place = jnp.stack([lax.axis_index(a) for a in ("y", "zh", "c", "zl")]).astype(jnp.int32)
    block_shape = shape((4, 4, balanced, width_local), bf16)
    column = shape((balanced, 1), f32)
    scaled_grad, table_all = call(
        gate_kernel,
        (block_shape, shape((tensor_count, 16, width_local), f32)),
        [],
        4 * US,
        0,
        place, gathered, member,
    )
    rows_all, first_other, last, scaled_grad = lax.optimization_barrier(
        (rows_all, first_other, last, scaled_grad)
    )
    last_other = shifted(last, "c", 1)
    weight_parts = (first, first_other, last, last_other)
    modulated, average, inv_scale = call(
        rows_kernel,
        (shape((4, 4, balanced + 16, width_local), bf16), column, column),
        [],
        6 * US,
        0,
        place, rows_all, table_all, member,
    )
    unit_rows = shape((hid, balanced), bf16)
    whole = lambda *dims: pl.BlockSpec(dims, lambda *_: (0,) * len(dims))
    by_dy = lambda *dims: pl.BlockSpec((1,) + dims, lambda dy, *_: (dy,) + (0,) * len(dims))
    params = pltpu.CompilerParams(vmem_limit_bytes=VMEM)
    planes = weights.shape[1:]
    hidden, pre_grad, sums = pl.pallas_call(
        hidden_kernel,
        grid=(4,),
        out_shape=(unit_rows, unit_rows, shape((16, balanced), bf16)),
        in_specs=[
            by_dy(4, balanced + 16, width_local),
            by_dy(4, balanced, width_local),
            whole(balanced, SAMPLES),
            by_dy(3, 2, *planes), by_dy(3, 2, *planes),
            by_dy(1, 2, *planes), by_dy(1, 2, *planes),
        ],
        out_specs=(whole(hid, balanced), whole(hid, balanced), whole(16, balanced)),
        scratch_shapes=[
            pltpu.VMEM((balanced + 16, hid), f32), pltpu.VMEM((balanced, hid), f32)
        ],
        compiler_params=params,
        cost_estimate=pl.CostEstimate(flops=8 * US, bytes_accessed=0, transcendentals=0),
    )(modulated, scaled_grad, member, *weight_parts)

    def outward(which, units, *extra):
        pick = lambda n: pl.BlockSpec(
            (1, n, 1) + planes, lambda dy, _: (dy, 0, which, 0, 0)
        )
        height = width_local + sum(e.shape[0] for e in extra)
        return pl.pallas_call(
            outward_kernel,
            grid_spec=pltpu.PrefetchScalarGridSpec(
                num_scalar_prefetch=1,
                grid=(4,),
                in_specs=[whole(hid, balanced), pick(3), pick(3), pick(1), pick(1)]
                + [whole(*e.shape) for e in extra],
                out_specs=pl.BlockSpec(
                    (1, 4, height, balanced),
                    lambda dy, at: (lax.rem(at[0] - dy + 4, 4), 0, 0, 0),
                ),
            ),
            out_shape=shape((4, 4, height, balanced), bf16),
            compiler_params=params,
            cost_estimate=pl.CostEstimate(flops=5 * US, bytes_accessed=0, transcendentals=0),
        )(place, units, *weight_parts, *extra)

    partial_in = outward(0, pre_grad, sums)
    partial_out = outward(1, hidden)

    from_x = lax.all_to_all(partial_in, "x", split_axis=0, concat_axis=0, tiled=True)
    from_x, partial_out = lax.optimization_barrier((from_x, partial_out))
    out_x = lax.all_to_all(partial_out, "x", split_axis=0, concat_axis=0, tiled=True)
    (in_x,) = call(fold_kernel, (shape(partial_in.shape[1:], bf16),), [], 2 * US, 0, place, from_x)
    in_zl = [in_x[0]] + [shifted(in_x[k], "zl", k) for k in (1, 2, 3)]
    out_x, in_zl = lax.optimization_barrier((out_x, in_zl))
    out_x, totals_zl = call(
        fold_kernel,
        (shape(partial_out.shape[1:], bf16), shape((4, SAMPLES, width_local), f32)),
        [], 3 * US, 0,
        place, out_x, grad_zl, member,
    )
    totals_out = totals_zl[0]
    for k in (1, 2, 3):
        totals_out = totals_out + shifted(totals_zl[k], "zl", k)

    source_rows = ((position - row_starts[:, None]) & low) + groups * slot_ids
    back_index = jnp.where(
        source_rows < live_rows[:, None],
        (row_starts[:, None] + source_rows - position) >> bits,
        -1,
    ).reshape(-1, 1)
    returning, totals_in = call(
        functools.partial(finish_in_kernel, model_width),
        (shape((slots_in, width_local), bf16), shape((2 * SAMPLES, width_local), f32)),
        [], 4 * US, 0,
        *in_zl, rows_bal, out_grad, average, inv_scale, member, table, back_index,
    )
    returning = returning.reshape(groups, per_pair, width_local)
    arrived = lax.all_to_all(returning, DP, split_axis=0, concat_axis=0, tiled=True)

    mod_grad = summed(jnp.concatenate([totals_in, totals_out], axis=0), "c")
    mod_grad, out_x = lax.optimization_barrier((mod_grad, out_x))
    mod_grad = summed(summed(mod_grad, "y"), "zh").reshape(modulation.shape)
    out_zl = [out_x[0]] + [shifted(out_x[k], "zl", k) for k in (1, 2, 3)]
    (block_out,) = call(
        finish_out_kernel, (shape((balanced, width_local), bf16),), [], 2 * US, 0,
        *out_zl, rows_bal, member, table,
    )

    own_rows = jnp.arange(slots_in, dtype=jnp.int32)
    target = ((own_start + own_rows) & low) * per_pair + (own_rows >> bits)
    target = jnp.where(own_rows < own_live, target, -1).reshape(-1, 1)
    (input_grad,) = call(
        pick_kernel, (shape((slots_in, width_local), bf16),), [], 2 * US, 0,
        target, arrived.reshape(slots_in, width_local),
    )
    return (block_out, input_grad, mod_grad)


def solution(mesh):
    cut = Mesh(mesh.devices.reshape(SIZES), AXES)
    return jax.shard_map(
        body,
        mesh=cut,
        in_specs=(
            P(DP, TP),
            P(),
            P(),
            P(DP, TP),
            P(TP, DP),
            P(None, None, TP),
            P(DP, TP),
        ),
        out_specs=(P(DP, TP), P(DP, TP), P(None, None, TP)),
        check_vma=False,
    )
```

```python
import functools

import jax
import jax.numpy as jnp
from jax import lax
from jax.experimental import pallas as pl
from jax.experimental.pallas import tpu as pltpu
from jax.sharding import Mesh, PartitionSpec as P

GELU_K = 0.7978845608028654
GELU_C = 0.044715
EPS = 1e-06
AXES = ("zh", "y", "c", "zl", "x")
SIZES = (4, 4, 2, 4, 4)
DP = ("zh", "y", "c")
TP = ("zl", "x")
SAMPLES = 4
VMEM = 48 * 1024 * 1024
US = 10**9


def gelu_value(pre):
    inner = GELU_K * (pre + GELU_C * pre * pre * pre)
    return 0.5 * pre * (1.0 + jnp.tanh(inner))


def gelu_slope(pre):
    inner = GELU_K * (pre + GELU_C * pre * pre * pre)
    tangent = jnp.tanh(inner)
    return 0.5 * (1.0 + tangent) + 0.5 * pre * (1.0 - tangent * tangent) * GELU_K * (
        1.0 + 3.0 * GELU_C * pre * pre
    )


def shifted(value, axis, step):
    size = lax.axis_size(axis)
    return lax.ppermute(value, axis, [(i, (i + step) % size) for i in range(size)])


def crossed(value, axis, mask):
    size = lax.axis_size(axis)
    return lax.ppermute(value, axis, [(i, i ^ mask) for i in range(size)])


def direct_pieces(value, axis):
    return jnp.stack([value] + [shifted(value, axis, k) for k in (1, 2, 3)])


def spread(value, axis):
    copies = jnp.broadcast_to(value[None], (lax.axis_size(axis),) + value.shape)
    return lax.all_to_all(copies, axis, split_axis=0, concat_axis=0, tiled=True)


def summed(value, axis):
    mask = 1
    while mask < lax.axis_size(axis):
        value = value + crossed(value, axis, mask)
        mask *= 2
    return value


def three_terms(value):
    terms = []
    for _ in range(3):
        term = lax.reduce_precision(value, 8, 7)
        terms.append(term.astype(jnp.bfloat16))
        value = value - term
    return terms


def sample_mix(member, table):
    out = jnp.broadcast_to(table[SAMPLES - 1 : SAMPLES], (member.shape[0], table.shape[1]))
    for q in range(SAMPLES - 1):
        out = jnp.where(member[:, q : q + 1] > 0.5, table[q : q + 1], out)
    return out


def halves(c, half):
    first = pl.ds(pl.multiple_of(c * half, half), half)
    second = pl.ds(pl.multiple_of((1 - c) * half, half), half)
    return first, second


def zh_of(zh, n, count):
    step = jnp.where(n == 1, count - 1, jnp.where(n == 2, 1, jnp.where(n == 3, 2, 0)))
    return lax.rem(zh + step, count)


def weight_of(parts, n, which):
    group, place = ((0, 0), (1, 0), (1, 1), (2, 0))[n]
    return jnp.concatenate(
        [parts[group][0, place, which], parts[3 + group][0, place, which]], axis=0
    )


def gate_kernel(place, gathered, member, grad_out, table_out):
    y, zh, c = place[0], place[1], place[2]
    live = member[...]
    count = grad_out.shape[0]
    rows = grad_out.shape[2]
    half = grad_out.shape[3] // 2

    def step(index, carry):
        dy, n = index // count, index % count
        xi = lax.rem(y - dy + count, count)
        zi = zh_of(zh, n, count)
        block = zi * count + xi
        terms = gathered[block, rows : rows + 48].astype(jnp.float32)
        table = (terms[0:16] + terms[16:32]) + terms[32:48]
        table_out[block] = table
        grad = gathered[block, 0:rows].astype(jnp.float32)
        gated = (sample_mix(live, table[8:12]) * grad).astype(jnp.bfloat16)
        first, second = halves(c, half)
        grad_out[dy, n, :, first] = gated[:, :half]
        grad_out[dy, n, :, second] = gated[:, half:]
        return carry

    lax.fori_loop(0, count * count, step, 0)


def rows_kernel(place, rows, table_in, member, mod_out, average, inv_scale):
    y, zh, c = place[0], place[1], place[2]
    live = member[...]
    count = rows.shape[0]
    balanced = rows.shape[2]
    width = rows.shape[3]
    half = width // 2
    features = count * count * width

    total = jnp.zeros(rows.shape[2:], jnp.float32)
    for i in range(count):
        for j in range(count):
            total = total + rows[i, j].astype(jnp.float32)
    mean = jnp.sum(total, axis=1, keepdims=True) / features
    total = jnp.zeros(rows.shape[2:], jnp.float32)
    for i in range(count):
        for j in range(count):
            centred = rows[i, j].astype(jnp.float32) - mean
            total = total + centred * centred
    inv = lax.rsqrt(jnp.sum(total, axis=1, keepdims=True) / features + EPS)
    average[...] = mean
    inv_scale[...] = inv

    def step(index, carry):
        dy, n = index // count, index % count
        xi = lax.rem(y - dy + count, count)
        zi = zh_of(zh, n, count)
        table = table_in[zi * count + xi]
        shift, scale = table[0:4], 1.0 + table[4:8]
        normed = (rows[xi, zi].astype(jnp.float32) - mean) * inv
        value = (normed * sample_mix(live, scale) + sample_mix(live, shift)).astype(jnp.bfloat16)
        scale_hi = scale.astype(jnp.bfloat16).astype(jnp.float32)
        shift_hi = shift.astype(jnp.bfloat16).astype(jnp.float32)
        extra = jnp.concatenate(
            [scale_hi, scale - scale_hi, shift_hi, shift - shift_hi], axis=0
        ).astype(jnp.bfloat16)
        first, second = halves(c, half)
        mod_out[dy, n, 0:balanced, first] = value[:, :half]
        mod_out[dy, n, 0:balanced, second] = value[:, half:]
        mod_out[dy, n, balanced : balanced + 16, first] = extra[:, :half]
        mod_out[dy, n, balanced : balanced + 16, second] = extra[:, half:]
        return carry

    lax.fori_loop(0, count * count, step, 0)


def hidden_kernel(
    modulated, scaled, member, part0, part1, part2, part3, part4, part5,
    hidden_out, pre_grad_out, sums_out, pre_total, grad_total,
):
    parts = (part0, part1, part2, part3, part4, part5)
    live = member[...]
    rows = scaled.shape[2]
    step = pl.program_id(0)

    @pl.when(step == 0)
    def _():
        pre_total[...] = jnp.zeros_like(pre_total)
        grad_total[...] = jnp.zeros_like(grad_total)

    for n in range(scaled.shape[1]):
        up = weight_of(parts, n, 0)
        pre_total[...] += jnp.dot(modulated[0, n], up, preferred_element_type=jnp.float32)
        down = weight_of(parts, n, 1)
        grad_total[...] += jnp.dot(scaled[0, n], down, preferred_element_type=jnp.float32)

    @pl.when(step == pl.num_programs(0) - 1)
    def _():
        pre = pre_total[0:rows]
        extra = pre_total[rows : rows + 16]
        hidden_out[...] = gelu_value(pre).astype(jnp.bfloat16).T
        pre_grad = (grad_total[...] * gelu_slope(pre)).astype(jnp.bfloat16)
        pre_grad_out[...] = pre_grad.T
        pre_grad = pre_grad.astype(jnp.float32)
        scale_part = sample_mix(live, extra[0:4] + extra[4:8])
        shift_part = sample_mix(live, extra[8:12] + extra[12:16])
        first = jnp.sum(pre_grad * scale_part, axis=1, keepdims=True)
        second = jnp.sum(pre_grad * (pre - shift_part), axis=1, keepdims=True)
        lane = lax.broadcasted_iota(jnp.int32, (rows, 128), 1)
        both = jnp.where(lane == 0, first, jnp.where(lane == 1, second, 0.0))
        sums = both.T[0:8]
        high = sums.astype(jnp.bfloat16).astype(jnp.float32)
        sums_out[...] = jnp.concatenate([high, sums - high], axis=0).astype(jnp.bfloat16)


def outward_kernel(place, hidden, *refs):
    out = refs[-1]
    zh, c = place[1], place[2]
    count = out.shape[1]
    rows = out.shape[3]
    half = rows // 2
    low, high = halves(c, half)
    for n in range(count):
        weight = weight_of(refs[:6], n, 0)
        value = jnp.dot(weight, hidden[...], preferred_element_type=jnp.float32).astype(
            jnp.bfloat16
        )
        zi = zh_of(zh, n, count)
        out[0, zi, low, :] = value[:half]
        out[0, zi, high, :] = value[half:]
        if len(refs) == 8:
            out[0, zi, rows : rows + 16, :] = refs[6][...]


def joined_sums(terms):
    total = terms[0:8] + terms[8:16]
    high = total.astype(jnp.bfloat16).astype(jnp.float32)
    return jnp.concatenate([high, total - high], axis=0)


def fold_kernel(place, blocks, out):
    count, places, height, width = blocks.shape

    def step(m, carry):
        total = blocks[0, m].astype(jnp.float32)
        for k in range(1, count):
            total = total + blocks[k, m].astype(jnp.float32)
        out[m, 0:width] = total[0:width].astype(jnp.bfloat16)
        out[m, width:height] = joined_sums(total[width:height]).astype(jnp.bfloat16)
        return carry

    lax.fori_loop(0, places, step, 0)


def fold_out_kernel(place, blocks, grad, member, out):
    zl = place[3]
    count, places, width, _ = blocks.shape

    def step(m, carry):
        total = blocks[0, m].astype(jnp.float32)
        for k in range(1, count):
            total = total + blocks[k, m].astype(jnp.float32)
        to = lax.rem(m - zl + places, places)
        out[to, 0:width] = total.astype(jnp.bfloat16)
        part = image_sums(member[...], grad[m].astype(jnp.float32) * total.T)
        part = jnp.concatenate(part, axis=0)
        high = part.astype(jnp.bfloat16).astype(jnp.float32)
        middle = (part - high).astype(jnp.bfloat16).astype(jnp.float32)
        low = (part - high) - middle
        terms = jnp.concatenate([high, middle, low, jnp.zeros_like(low)], axis=0)
        out[to, width : width + 16] = terms.astype(jnp.bfloat16)
        return carry

    lax.fori_loop(0, places, step, 0)


def picked(index, values):
    lanes = lax.broadcasted_iota(jnp.int32, (index.shape[0], values.shape[0]), 1)
    chosen = jnp.where(lanes == index, 1.0, 0.0).astype(jnp.bfloat16)
    return jnp.dot(chosen, values, preferred_element_type=jnp.float32).astype(jnp.bfloat16)


def image_sums(live, values):
    return [
        jnp.sum(jnp.where(live[:, q : q + 1] > 0.5, values, 0.0), axis=0, keepdims=True)
        for q in range(SAMPLES)
    ]


def finish_in_kernel(
    features, pieces, rows, grad, average, inv_scale, member, table, index, back, totals
):
    live = member[...]
    balanced = rows.shape[0]
    total = pieces[0].astype(jnp.float32)
    for k in range(1, pieces.shape[0]):
        total = total + pieces[k].astype(jnp.float32)
    mod_in_grad = total[0:balanced].T
    sums = total[balanced : balanced + 8] + total[balanced + 8 : balanced + 16]
    means = jnp.concatenate([sums, jnp.zeros((120, balanced), jnp.float32)], axis=0).T / features
    inv = inv_scale[...]
    normed = (rows[...].astype(jnp.float32) - average[...]) * inv
    normed_grad = mod_in_grad * (1.0 + sample_mix(live, table[4:8]))
    row_grad = grad[...].astype(jnp.float32) + inv * (
        normed_grad - means[:, 0:1] - normed * means[:, 1:2]
    )
    back[...] = picked(index[...], row_grad.astype(jnp.bfloat16))
    totals[...] = jnp.concatenate(
        image_sums(live, mod_in_grad) + image_sums(live, mod_in_grad * normed), axis=0
    )


def finish_out_kernel(piece0, piece1, piece2, piece3, rows, member, table, out):
    live = member[...]
    balanced = rows.shape[0]
    branch = piece0[0:balanced].astype(jnp.float32)
    for piece in (piece1, piece2, piece3):
        branch = branch + piece[0:balanced].astype(jnp.float32)
    branch = branch.T
    gate = sample_mix(live, table[8:12])
    out[...] = (rows[...].astype(jnp.float32) + gate * branch).astype(jnp.bfloat16)


def pick_kernel(index, values, out):
    out[...] = picked(index[...], values[...])


SMEM_SPEC = pl.BlockSpec(memory_space=pltpu.SMEM)
VMEM_SPEC = pl.BlockSpec(memory_space=pltpu.VMEM)


def call(kernel, outs, scratch, flops, moved, *args):
    return pl.pallas_call(
        kernel,
        out_shape=outs,
        in_specs=[SMEM_SPEC if a.ndim == 1 else VMEM_SPEC for a in args],
        out_specs=jax.tree.map(lambda _: VMEM_SPEC, outs),
        scratch_shapes=scratch,
        compiler_params=pltpu.CompilerParams(vmem_limit_bytes=VMEM),
        cost_estimate=pl.CostEstimate(flops=flops, bytes_accessed=moved, transcendentals=0),
    )(*args)


def body(hidden_in, live_rows, sample_tokens, w_up, w_down, modulation, out_grad):
    groups = lax.axis_size(DP)
    position = lax.axis_index(DP)
    slots_in = hidden_in.shape[0]
    per_pair = slots_in // groups
    balanced = out_grad.shape[0]
    width_local = hidden_in.shape[1]
    tensor_count = lax.axis_size(TP)
    model_width = width_local * tensor_count
    hid = w_up.shape[1]
    f32, bf16 = jnp.float32, jnp.bfloat16
    shape = jax.ShapeDtypeStruct
    low = groups - 1
    bits = groups.bit_length() - 1

    weights = jnp.stack([w_up, w_down.T])
    before = shifted(weights, "zh", 1)
    after = shifted(weights, "zh", -1)
    near = direct_pieces(weights[None], "y")

    table = modulation.reshape(-1, width_local)
    pad = jnp.zeros((16 - table.shape[0], width_local), f32)
    payload = jnp.concatenate([out_grad] + three_terms(jnp.concatenate([table, pad])), axis=0)

    row_ends = jnp.cumsum(live_rows)
    row_starts = row_ends - live_rows
    device_ids = jnp.arange(groups, dtype=jnp.int32)
    own_start = jnp.sum(jnp.where(device_ids < position, live_rows, 0))
    own_live = jnp.sum(jnp.where(device_ids == position, live_rows, 0))
    slot_ids = jnp.arange(per_pair, dtype=jnp.int32)[None, :]
    local_rows = ((device_ids[:, None] - own_start) & low) + groups * slot_ids
    outgoing = hidden_in[local_rows.reshape(-1)].reshape(groups, per_pair, width_local)
    gathered = lax.all_gather(payload, TP, axis=0)
    incoming = lax.all_to_all(outgoing, DP, split_axis=0, concat_axis=0, tiled=True)
    global_rows = position + groups * jnp.arange(balanced, dtype=jnp.int32)
    before_row = row_ends[None, :] <= global_rows[:, None]
    owners = jnp.sum(before_row.astype(jnp.int32), axis=1)
    owner_start = jnp.sum(jnp.where(before_row, live_rows[None, :], 0), axis=1)
    owner_slot = (global_rows - owner_start) >> bits
    incoming, before, after, near = lax.optimization_barrier((incoming, before, after, near))
    far = jnp.concatenate([shifted(before[:1], "zh", 1), shifted(after[1:], "zh", -1)], axis=0)
    pair = direct_pieces(jnp.stack([before, after]), "y")
    rows_bal = incoming.reshape(groups * per_pair, width_local)[owners * per_pair + owner_slot]
    sample_ends = jnp.cumsum(sample_tokens)
    sample_starts = sample_ends - sample_tokens
    member = (
        (global_rows[:, None] >= sample_starts[None, :])
        & (global_rows[:, None] < sample_ends[None, :])
    ).astype(f32)

    rows_zl = spread(rows_bal, "zl")
    rows_zl, far, pair, gathered = lax.optimization_barrier((rows_zl, far, pair, gathered))
    last = direct_pieces(far[None], "y")
    near_other = shifted(near, "c", 1)
    pair_other = shifted(pair, "c", 1)
    rows_all = spread(rows_zl, "x")

    by_place = gathered.reshape(4, 4, -1, width_local)
    grad_zl = lax.dynamic_index_in_dim(by_place, lax.axis_index("x"), 1, keepdims=False)
    grad_zl = grad_zl[:, :balanced]
    place = jnp.stack([lax.axis_index(a) for a in ("y", "zh", "c", "zl")]).astype(jnp.int32)
    block_shape = shape((4, 4, balanced, width_local), bf16)
    column = shape((balanced, 1), f32)
    scaled_grad, table_all = call(
        gate_kernel,
        (block_shape, shape((tensor_count, 16, width_local), f32)),
        [],
        4 * US,
        0,
        place, gathered, member,
    )
    rows_all, near_other, pair_other, last, scaled_grad = lax.optimization_barrier(
        (rows_all, near_other, pair_other, last, scaled_grad)
    )
    last_other = shifted(last, "c", 1)
    weight_parts = (near, pair, last, near_other, pair_other, last_other)
    modulated, average, inv_scale = call(
        rows_kernel,
        (shape((4, 4, balanced + 16, width_local), bf16), column, column),
        [],
        6 * US,
        0,
        place, rows_all, table_all, member,
    )
    unit_rows = shape((hid, balanced), bf16)
    whole = lambda *dims: pl.BlockSpec(dims, lambda *_: (0,) * len(dims))
    by_dy = lambda *dims: pl.BlockSpec((1,) + dims, lambda dy, *_: (dy,) + (0,) * len(dims))
    params = pltpu.CompilerParams(vmem_limit_bytes=VMEM)
    planes = weights.shape[1:]
    hidden, pre_grad, sums = pl.pallas_call(
        hidden_kernel,
        grid=(4,),
        out_shape=(unit_rows, unit_rows, shape((16, balanced), bf16)),
        in_specs=[
            by_dy(4, balanced + 16, width_local),
            by_dy(4, balanced, width_local),
            whole(balanced, SAMPLES),
        ]
        + [by_dy(n, 2, *planes) for n in (1, 2, 1)] * 2,
        out_specs=(whole(hid, balanced), whole(hid, balanced), whole(16, balanced)),
        scratch_shapes=[
            pltpu.VMEM((balanced + 16, hid), f32), pltpu.VMEM((balanced, hid), f32)
        ],
        compiler_params=params,
        cost_estimate=pl.CostEstimate(flops=8 * US, bytes_accessed=0, transcendentals=0),
    )(modulated, scaled_grad, member, *weight_parts)

    def outward(which, units, *extra):
        pick = lambda n: pl.BlockSpec(
            (1, n, 1) + planes, lambda dy, _: (dy, 0, which, 0, 0)
        )
        height = width_local + sum(e.shape[0] for e in extra)
        return pl.pallas_call(
            outward_kernel,
            grid_spec=pltpu.PrefetchScalarGridSpec(
                num_scalar_prefetch=1,
                grid=(4,),
                in_specs=[whole(hid, balanced)]
                + [pick(n) for n in (1, 2, 1)] * 2
                + [whole(*e.shape) for e in extra],
                out_specs=pl.BlockSpec(
                    (1, 4, height, balanced),
                    lambda dy, at: (lax.rem(at[0] - dy + 4, 4), 0, 0, 0),
                ),
            ),
            out_shape=shape((4, 4, height, balanced), bf16),
            compiler_params=params,
            cost_estimate=pl.CostEstimate(flops=5 * US, bytes_accessed=0, transcendentals=0),
        )(place, units, *weight_parts, *extra)

    partial_out = outward(1, hidden)
    partial_in = outward(0, pre_grad, sums)
    out_x = lax.all_to_all(partial_out, "x", split_axis=0, concat_axis=0, tiled=True)
    out_x, partial_in = lax.optimization_barrier((out_x, partial_in))
    in_x = lax.all_to_all(partial_in, "x", split_axis=0, concat_axis=0, tiled=True)
    (out_x,) = call(
        fold_out_kernel, (shape((4, width_local + 16, balanced), bf16),), [], 3 * US, 0,
        place, out_x, grad_zl, member,
    )
    out_zl = [out_x[0]] + [shifted(out_x[k], "zl", k) for k in (1, 2, 3)]
    in_x, out_zl = lax.optimization_barrier((in_x, out_zl))
    terms = jnp.sum(jnp.stack([o[width_local : width_local + 12] for o in out_zl]).astype(f32), 0)
    totals_out = (terms[0:4] + terms[4:8]) + terms[8:12]
    (in_x,) = call(fold_kernel, (shape(partial_in.shape[1:], bf16),), [], 2 * US, 0, place, in_x)
    in_zl = lax.all_to_all(in_x, "zl", split_axis=0, concat_axis=0, tiled=True)

    source_rows = ((position - row_starts[:, None]) & low) + groups * slot_ids
    back_index = jnp.where(
        source_rows < live_rows[:, None],
        (row_starts[:, None] + source_rows - position) >> bits,
        -1,
    ).reshape(-1, 1)
    returning, totals_in = call(
        functools.partial(finish_in_kernel, model_width),
        (shape((slots_in, width_local), bf16), shape((2 * SAMPLES, width_local), f32)),
        [], 4 * US, 0,
        in_zl, rows_bal, out_grad, average, inv_scale, member, table, back_index,
    )
    returning = returning.reshape(groups, per_pair, width_local)
    arrived = lax.all_to_all(returning, DP, split_axis=0, concat_axis=0, tiled=True)

    mod_grad = jnp.concatenate([totals_in, totals_out], axis=0)
    mod_grad = summed(summed(summed(mod_grad, "c"), "y"), "zh").reshape(modulation.shape)
    (block_out,) = call(
        finish_out_kernel, (shape((balanced, width_local), bf16),), [], 2 * US, 0,
        *out_zl, rows_bal, member, table,
    )

    own_rows = jnp.arange(slots_in, dtype=jnp.int32)
    target = ((own_start + own_rows) & low) * per_pair + (own_rows >> bits)
    target = jnp.where(own_rows < own_live, target, -1).reshape(-1, 1)
    (input_grad,) = call(
        pick_kernel, (shape((slots_in, width_local), bf16),), [], 2 * US, 0,
        target, arrived.reshape(slots_in, width_local),
    )
    return (block_out, input_grad, mod_grad)


def solution(mesh):
    cut = Mesh(mesh.devices.reshape(SIZES), AXES)
    return jax.shard_map(
        body,
        mesh=cut,
        in_specs=(
            P(DP, TP),
            P(),
            P(),
            P(DP, TP),
            P(TP, DP),
            P(None, None, TP),
            P(DP, TP),
        ),
        out_specs=(P(DP, TP), P(DP, TP), P(None, None, TP)),
        check_vma=False,
    )
```

```python
import functools

import jax
import jax.numpy as jnp
from jax import lax
from jax.experimental import pallas as pl
from jax.experimental.pallas import tpu as pltpu
from jax.sharding import Mesh, PartitionSpec as P

GELU_K = 0.7978845608028654
GELU_C = 0.044715
EPS = 1e-06
AXES = ("zh", "y", "c", "zl", "x")
SIZES = (4, 4, 2, 4, 4)
DP = ("zh", "y", "c")
TP = ("zl", "x")
SAMPLES = 4
VMEM = 48 * 1024 * 1024
US = 10**9


def gelu_value(pre):
    inner = GELU_K * (pre + GELU_C * pre * pre * pre)
    return 0.5 * pre * (1.0 + jnp.tanh(inner))


def gelu_slope(pre):
    inner = GELU_K * (pre + GELU_C * pre * pre * pre)
    tangent = jnp.tanh(inner)
    return 0.5 * (1.0 + tangent) + 0.5 * pre * (1.0 - tangent * tangent) * GELU_K * (
        1.0 + 3.0 * GELU_C * pre * pre
    )


def shifted(value, axis, step):
    size = lax.axis_size(axis)
    return lax.ppermute(value, axis, [(i, (i + step) % size) for i in range(size)])


def crossed(value, axis, mask):
    size = lax.axis_size(axis)
    return lax.ppermute(value, axis, [(i, i ^ mask) for i in range(size)])


def direct_pieces(value, axis):
    return jnp.stack([value] + [shifted(value, axis, k) for k in (1, 2, 3)])


def spread(value, axis):
    copies = jnp.broadcast_to(value[None], (lax.axis_size(axis),) + value.shape)
    return lax.all_to_all(copies, axis, split_axis=0, concat_axis=0, tiled=True)


def summed(value, axis):
    mask = 1
    while mask < lax.axis_size(axis):
        value = value + crossed(value, axis, mask)
        mask *= 2
    return value


def three_terms(value):
    terms = []
    for _ in range(3):
        term = lax.reduce_precision(value, 8, 7)
        terms.append(term.astype(jnp.bfloat16))
        value = value - term
    return terms


def sample_mix(member, table):
    out = jnp.broadcast_to(table[SAMPLES - 1 : SAMPLES], (member.shape[0], table.shape[1]))
    for q in range(SAMPLES - 1):
        out = jnp.where(member[:, q : q + 1] > 0.5, table[q : q + 1], out)
    return out


def halves(c, half):
    first = pl.ds(pl.multiple_of(c * half, half), half)
    second = pl.ds(pl.multiple_of((1 - c) * half, half), half)
    return first, second


def zh_of(zh, n, count):
    step = jnp.where(n == 1, count - 1, jnp.where(n == 2, 1, jnp.where(n == 3, 2, 0)))
    return lax.rem(zh + step, count)


def weight_of(parts, n, which):
    group, place = ((0, 0), (1, 0), (1, 1), (2, 0))[n]
    return jnp.concatenate(
        [parts[group][0, place, which], parts[3 + group][0, place, which]], axis=0
    )


def gate_kernel(place, gathered, member, grad_out, table_out):
    y, zh, c = place[0], place[1], place[2]
    live = member[...]
    count = grad_out.shape[0]
    rows = grad_out.shape[2]
    half = grad_out.shape[3] // 2

    def step(index, carry):
        dy, n = index // count, index % count
        xi = lax.rem(y - dy + count, count)
        zi = zh_of(zh, n, count)
        block = zi * count + xi
        terms = gathered[block, rows : rows + 48].astype(jnp.float32)
        table = (terms[0:16] + terms[16:32]) + terms[32:48]
        table_out[block] = table
        grad = gathered[block, 0:rows].astype(jnp.float32)
        gated = (sample_mix(live, table[8:12]) * grad).astype(jnp.bfloat16)
        first, second = halves(c, half)
        grad_out[dy, n, :, first] = gated[:, :half]
        grad_out[dy, n, :, second] = gated[:, half:]
        return carry

    lax.fori_loop(0, count * count, step, 0)


def rows_kernel(place, rows, table_in, member, mod_out, average, inv_scale):
    y, zh, c = place[0], place[1], place[2]
    live = member[...]
    count = rows.shape[0]
    balanced = rows.shape[2]
    width = rows.shape[3]
    half = width // 2
    features = count * count * width

    total = jnp.zeros(rows.shape[2:], jnp.float32)
    for i in range(count):
        for j in range(count):
            total = total + rows[i, j].astype(jnp.float32)
    mean = jnp.sum(total, axis=1, keepdims=True) / features
    total = jnp.zeros(rows.shape[2:], jnp.float32)
    for i in range(count):
        for j in range(count):
            centred = rows[i, j].astype(jnp.float32) - mean
            total = total + centred * centred
    inv = lax.rsqrt(jnp.sum(total, axis=1, keepdims=True) / features + EPS)
    average[...] = mean
    inv_scale[...] = inv

    def step(index, carry):
        dy, n = index // count, index % count
        xi = lax.rem(y - dy + count, count)
        zi = zh_of(zh, n, count)
        table = table_in[zi * count + xi]
        shift, scale = table[0:4], 1.0 + table[4:8]
        normed = (rows[xi, zi].astype(jnp.float32) - mean) * inv
        value = (normed * sample_mix(live, scale) + sample_mix(live, shift)).astype(jnp.bfloat16)
        scale_hi = scale.astype(jnp.bfloat16).astype(jnp.float32)
        shift_hi = shift.astype(jnp.bfloat16).astype(jnp.float32)
        extra = jnp.concatenate(
            [scale_hi, scale - scale_hi, shift_hi, shift - shift_hi], axis=0
        ).astype(jnp.bfloat16)
        first, second = halves(c, half)
        mod_out[dy, n, 0:balanced, first] = value[:, :half]
        mod_out[dy, n, 0:balanced, second] = value[:, half:]
        mod_out[dy, n, balanced : balanced + 16, first] = extra[:, :half]
        mod_out[dy, n, balanced : balanced + 16, second] = extra[:, half:]
        return carry

    lax.fori_loop(0, count * count, step, 0)


def hidden_kernel(
    modulated, scaled, member, part0, part1, part2, part3, part4, part5,
    hidden_out, pre_grad_out, sums_out, pre_total, grad_total,
):
    parts = (part0, part1, part2, part3, part4, part5)
    live = member[...]
    rows = scaled.shape[2]
    step = pl.program_id(0)

    @pl.when(step == 0)
    def _():
        pre_total[...] = jnp.zeros_like(pre_total)
        grad_total[...] = jnp.zeros_like(grad_total)

    for n in range(scaled.shape[1]):
        up = weight_of(parts, n, 0)
        pre_total[...] += jnp.dot(modulated[0, n], up, preferred_element_type=jnp.float32)
        down = weight_of(parts, n, 1)
        grad_total[...] += jnp.dot(scaled[0, n], down, preferred_element_type=jnp.float32)

    @pl.when(step == pl.num_programs(0) - 1)
    def _():
        pre = pre_total[0:rows]
        extra = pre_total[rows : rows + 16]
        hidden_out[...] = gelu_value(pre).astype(jnp.bfloat16).T
        pre_grad = (grad_total[...] * gelu_slope(pre)).astype(jnp.bfloat16)
        pre_grad_out[...] = pre_grad.T
        pre_grad = pre_grad.astype(jnp.float32)
        scale_part = sample_mix(live, extra[0:4] + extra[4:8])
        shift_part = sample_mix(live, extra[8:12] + extra[12:16])
        first = jnp.sum(pre_grad * scale_part, axis=1, keepdims=True)
        second = jnp.sum(pre_grad * (pre - shift_part), axis=1, keepdims=True)
        lane = lax.broadcasted_iota(jnp.int32, (rows, 128), 1)
        both = jnp.where(lane == 0, first, jnp.where(lane == 1, second, 0.0))
        sums = both.T[0:8]
        high = sums.astype(jnp.bfloat16).astype(jnp.float32)
        sums_out[...] = jnp.concatenate([high, sums - high], axis=0).astype(jnp.bfloat16)


def outward_kernel(place, hidden, *refs):
    out = refs[-1]
    zh, c = place[1], place[2]
    count = out.shape[1]
    rows = out.shape[3]
    half = rows // 2
    low, high = halves(c, half)
    for n in range(count):
        weight = weight_of(refs[:6], n, 0)
        value = jnp.dot(weight, hidden[...], preferred_element_type=jnp.float32).astype(
            jnp.bfloat16
        )
        zi = zh_of(zh, n, count)
        out[0, zi, low, :] = value[:half]
        out[0, zi, high, :] = value[half:]
        if len(refs) == 8:
            out[0, zi, rows : rows + 16, :] = refs[6][...]


def joined_sums(terms):
    total = terms[0:8] + terms[8:16]
    high = total.astype(jnp.bfloat16).astype(jnp.float32)
    return jnp.concatenate([high, total - high], axis=0)


def fold_kernel(place, blocks, out):
    count, places, height, width = blocks.shape

    def step(m, carry):
        total = blocks[0, m].astype(jnp.float32)
        for k in range(1, count):
            total = total + blocks[k, m].astype(jnp.float32)
        out[m, 0:width] = total[0:width].astype(jnp.bfloat16)
        out[m, width:height] = joined_sums(total[width:height]).astype(jnp.bfloat16)
        return carry

    lax.fori_loop(0, places, step, 0)


def fold_out_kernel(place, blocks, grad, member, out):
    zl = place[3]
    count, places, width, _ = blocks.shape

    def step(m, carry):
        total = blocks[0, m].astype(jnp.float32)
        for k in range(1, count):
            total = total + blocks[k, m].astype(jnp.float32)
        to = lax.rem(m - zl + places, places)
        out[to, 0:width] = total.astype(jnp.bfloat16)
        part = image_sums(member[...], grad[m].astype(jnp.float32) * total.T)
        part = jnp.concatenate(part, axis=0)
        high = part.astype(jnp.bfloat16).astype(jnp.float32)
        middle = (part - high).astype(jnp.bfloat16).astype(jnp.float32)
        low = (part - high) - middle
        terms = jnp.concatenate([high, middle, low, jnp.zeros_like(low)], axis=0)
        out[to, width : width + 16] = terms.astype(jnp.bfloat16)
        return carry

    lax.fori_loop(0, places, step, 0)


def picked(index, values):
    lanes = lax.broadcasted_iota(jnp.int32, (index.shape[0], values.shape[0]), 1)
    chosen = jnp.where(lanes == index, 1.0, 0.0).astype(jnp.bfloat16)
    return jnp.dot(chosen, values, preferred_element_type=jnp.float32).astype(jnp.bfloat16)


def image_sums(live, values):
    return [
        jnp.sum(jnp.where(live[:, q : q + 1] > 0.5, values, 0.0), axis=0, keepdims=True)
        for q in range(SAMPLES)
    ]


def finish_in_kernel(
    features, pieces, rows, grad, average, inv_scale, member, table, index, back, totals
):
    live = member[...]
    balanced = rows.shape[0]
    total = pieces[0].astype(jnp.float32)
    for k in range(1, pieces.shape[0]):
        total = total + pieces[k].astype(jnp.float32)
    mod_in_grad = total[0:balanced].T
    sums = total[balanced : balanced + 8] + total[balanced + 8 : balanced + 16]
    means = jnp.concatenate([sums, jnp.zeros((120, balanced), jnp.float32)], axis=0).T / features
    inv = inv_scale[...]
    normed = (rows[...].astype(jnp.float32) - average[...]) * inv
    normed_grad = mod_in_grad * (1.0 + sample_mix(live, table[4:8]))
    row_grad = grad[...].astype(jnp.float32) + inv * (
        normed_grad - means[:, 0:1] - normed * means[:, 1:2]
    )
    back[...] = picked(index[...], row_grad.astype(jnp.bfloat16))
    totals[...] = jnp.concatenate(
        image_sums(live, mod_in_grad) + image_sums(live, mod_in_grad * normed), axis=0
    )


def finish_out_kernel(piece0, piece1, piece2, piece3, rows, member, table, out):
    live = member[...]
    balanced = rows.shape[0]
    branch = piece0[0:balanced].astype(jnp.float32)
    for piece in (piece1, piece2, piece3):
        branch = branch + piece[0:balanced].astype(jnp.float32)
    branch = branch.T
    gate = sample_mix(live, table[8:12])
    out[...] = (rows[...].astype(jnp.float32) + gate * branch).astype(jnp.bfloat16)


def send_kernel(position, live_rows, values, out):
    groups = live_rows.shape[0]
    slots = values.shape[0] // groups
    start = jnp.int32(0)
    for i in range(groups):
        start = start + jnp.where(i < position[0], live_rows[i], 0)
    row = lax.broadcasted_iota(jnp.int32, (values.shape[0], 1), 0)
    device = (row * (65536 // slots + 1)) >> 16
    index = ((device - start) & (groups - 1)) + groups * (row - slots * device)
    out[...] = picked(index, values[...])


def pick_kernel(index, values, out):
    out[...] = picked(index[...], values[...])


SMEM_SPEC = pl.BlockSpec(memory_space=pltpu.SMEM)
VMEM_SPEC = pl.BlockSpec(memory_space=pltpu.VMEM)


def call(kernel, outs, scratch, flops, moved, *args):
    return pl.pallas_call(
        kernel,
        out_shape=outs,
        in_specs=[SMEM_SPEC if a.ndim == 1 else VMEM_SPEC for a in args],
        out_specs=jax.tree.map(lambda _: VMEM_SPEC, outs),
        scratch_shapes=scratch,
        compiler_params=pltpu.CompilerParams(vmem_limit_bytes=VMEM),
        cost_estimate=pl.CostEstimate(flops=flops, bytes_accessed=moved, transcendentals=0),
    )(*args)


def body(hidden_in, live_rows, sample_tokens, w_up, w_down, modulation, out_grad):
    groups = lax.axis_size(DP)
    position = lax.axis_index(DP)
    slots_in = hidden_in.shape[0]
    per_pair = slots_in // groups
    balanced = out_grad.shape[0]
    width_local = hidden_in.shape[1]
    tensor_count = lax.axis_size(TP)
    model_width = width_local * tensor_count
    hid = w_up.shape[1]
    f32, bf16 = jnp.float32, jnp.bfloat16
    shape = jax.ShapeDtypeStruct
    low = groups - 1
    bits = groups.bit_length() - 1

    weights = jnp.stack([w_up, w_down.T])
    before = shifted(weights, "zh", 1)
    after = shifted(weights, "zh", -1)
    near = direct_pieces(weights[None], "y")

    table = modulation.reshape(-1, width_local)
    pad = jnp.zeros((16 - table.shape[0], width_local), f32)
    payload = jnp.concatenate([out_grad] + three_terms(jnp.concatenate([table, pad])), axis=0)

    row_ends = jnp.cumsum(live_rows)
    row_starts = row_ends - live_rows
    device_ids = jnp.arange(groups, dtype=jnp.int32)
    own_start = jnp.sum(jnp.where(device_ids < position, live_rows, 0))
    own_live = jnp.sum(jnp.where(device_ids == position, live_rows, 0))
    slot_ids = jnp.arange(per_pair, dtype=jnp.int32)[None, :]
    (outgoing,) = call(
        send_kernel, (shape((slots_in, width_local), bf16),), [], 2 * US, 0,
        position.astype(jnp.int32).reshape(1), live_rows, hidden_in,
    )
    outgoing = outgoing.reshape(groups, per_pair, width_local)
    gathered = lax.all_gather(payload, TP, axis=0)
    incoming = lax.all_to_all(outgoing, DP, split_axis=0, concat_axis=0, tiled=True)
    global_rows = position + groups * jnp.arange(balanced, dtype=jnp.int32)
    before_row = row_ends[None, :] <= global_rows[:, None]
    owners = jnp.sum(before_row.astype(jnp.int32), axis=1)
    owner_start = jnp.sum(jnp.where(before_row, live_rows[None, :], 0), axis=1)
    owner_slot = (global_rows - owner_start) >> bits
    incoming, before, after, near = lax.optimization_barrier((incoming, before, after, near))
    far = jnp.concatenate([shifted(before[:1], "zh", 1), shifted(after[1:], "zh", -1)], axis=0)
    pair = direct_pieces(jnp.stack([before, after]), "y")
    rows_bal = incoming.reshape(groups * per_pair, width_local)[owners * per_pair + owner_slot]
    sample_ends = jnp.cumsum(sample_tokens)
    sample_starts = sample_ends - sample_tokens
    member = (
        (global_rows[:, None] >= sample_starts[None, :])
        & (global_rows[:, None] < sample_ends[None, :])
    ).astype(f32)

    rows_zl = spread(rows_bal, "zl")
    rows_zl, far, pair, gathered = lax.optimization_barrier((rows_zl, far, pair, gathered))
    last = direct_pieces(far[None], "y")
    near_other = shifted(near, "c", 1)
    pair_other = shifted(pair, "c", 1)
    rows_all = spread(rows_zl, "x")

    by_place = gathered.reshape(4, 4, -1, width_local)
    grad_zl = lax.dynamic_index_in_dim(by_place, lax.axis_index("x"), 1, keepdims=False)
    grad_zl = grad_zl[:, :balanced]
    place = jnp.stack([lax.axis_index(a) for a in ("y", "zh", "c", "zl")]).astype(jnp.int32)
    block_shape = shape((4, 4, balanced, width_local), bf16)
    column = shape((balanced, 1), f32)
    scaled_grad, table_all = call(
        gate_kernel,
        (block_shape, shape((tensor_count, 16, width_local), f32)),
        [],
        4 * US,
        0,
        place, gathered, member,
    )
    rows_all, near_other, pair_other, last, scaled_grad = lax.optimization_barrier(
        (rows_all, near_other, pair_other, last, scaled_grad)
    )
    last_other = shifted(last, "c", 1)
    weight_parts = (near, pair, last, near_other, pair_other, last_other)
    modulated, average, inv_scale = call(
        rows_kernel,
        (shape((4, 4, balanced + 16, width_local), bf16), column, column),
        [],
        6 * US,
        0,
        place, rows_all, table_all, member,
    )
    unit_rows = shape((hid, balanced), bf16)
    whole = lambda *dims: pl.BlockSpec(dims, lambda *_: (0,) * len(dims))
    by_dy = lambda *dims: pl.BlockSpec((1,) + dims, lambda dy, *_: (dy,) + (0,) * len(dims))
    params = pltpu.CompilerParams(vmem_limit_bytes=VMEM)
    planes = weights.shape[1:]
    hidden, pre_grad, sums = pl.pallas_call(
        hidden_kernel,
        grid=(4,),
        out_shape=(unit_rows, unit_rows, shape((16, balanced), bf16)),
        in_specs=[
            by_dy(4, balanced + 16, width_local),
            by_dy(4, balanced, width_local),
            whole(balanced, SAMPLES),
        ]
        + [by_dy(n, 2, *planes) for n in (1, 2, 1)] * 2,
        out_specs=(whole(hid, balanced), whole(hid, balanced), whole(16, balanced)),
        scratch_shapes=[
            pltpu.VMEM((balanced + 16, hid), f32), pltpu.VMEM((balanced, hid), f32)
        ],
        compiler_params=params,
        cost_estimate=pl.CostEstimate(flops=8 * US, bytes_accessed=0, transcendentals=0),
    )(modulated, scaled_grad, member, *weight_parts)

    def outward(which, units, *extra):
        pick = lambda n: pl.BlockSpec(
            (1, n, 1) + planes, lambda dy, _: (dy, 0, which, 0, 0)
        )
        height = width_local + sum(e.shape[0] for e in extra)
        return pl.pallas_call(
            outward_kernel,
            grid_spec=pltpu.PrefetchScalarGridSpec(
                num_scalar_prefetch=1,
                grid=(4,),
                in_specs=[whole(hid, balanced)]
                + [pick(n) for n in (1, 2, 1)] * 2
                + [whole(*e.shape) for e in extra],
                out_specs=pl.BlockSpec(
                    (1, 4, height, balanced),
                    lambda dy, at: (lax.rem(at[0] - dy + 4, 4), 0, 0, 0),
                ),
            ),
            out_shape=shape((4, 4, height, balanced), bf16),
            compiler_params=params,
            cost_estimate=pl.CostEstimate(flops=5 * US, bytes_accessed=0, transcendentals=0),
        )(place, units, *weight_parts, *extra)

    partial_out = outward(1, hidden)
    partial_in = outward(0, pre_grad, sums)
    out_x = lax.all_to_all(partial_out, "x", split_axis=0, concat_axis=0, tiled=True)
    out_x, partial_in = lax.optimization_barrier((out_x, partial_in))
    in_x = lax.all_to_all(partial_in, "x", split_axis=0, concat_axis=0, tiled=True)
    (out_x,) = call(
        fold_out_kernel, (shape((4, width_local + 16, balanced), bf16),), [], 3 * US, 0,
        place, out_x, grad_zl, member,
    )
    out_zl = [out_x[0]] + [shifted(out_x[k], "zl", k) for k in (1, 2, 3)]
    in_x, out_zl = lax.optimization_barrier((in_x, out_zl))
    terms = jnp.sum(jnp.stack([o[width_local : width_local + 12] for o in out_zl]).astype(f32), 0)
    totals_out = (terms[0:4] + terms[4:8]) + terms[8:12]
    (in_x,) = call(fold_kernel, (shape(partial_in.shape[1:], bf16),), [], 2 * US, 0, place, in_x)
    in_zl = lax.all_to_all(in_x, "zl", split_axis=0, concat_axis=0, tiled=True)

    source_rows = ((position - row_starts[:, None]) & low) + groups * slot_ids
    back_index = jnp.where(
        source_rows < live_rows[:, None],
        (row_starts[:, None] + source_rows - position) >> bits,
        -1,
    ).reshape(-1, 1)
    returning, totals_in = call(
        functools.partial(finish_in_kernel, model_width),
        (shape((slots_in, width_local), bf16), shape((2 * SAMPLES, width_local), f32)),
        [], 4 * US, 0,
        in_zl, rows_bal, out_grad, average, inv_scale, member, table, back_index,
    )
    returning = returning.reshape(groups, per_pair, width_local)
    arrived = lax.all_to_all(returning, DP, split_axis=0, concat_axis=0, tiled=True)

    mod_grad = jnp.concatenate([totals_in, totals_out], axis=0)
    mod_grad = summed(summed(summed(mod_grad, "c"), "y"), "zh").reshape(modulation.shape)
    (block_out,) = call(
        finish_out_kernel, (shape((balanced, width_local), bf16),), [], 2 * US, 0,
        *out_zl, rows_bal, member, table,
    )

    own_rows = jnp.arange(slots_in, dtype=jnp.int32)
    target = ((own_start + own_rows) & low) * per_pair + (own_rows >> bits)
    target = jnp.where(own_rows < own_live, target, -1).reshape(-1, 1)
    (input_grad,) = call(
        pick_kernel, (shape((slots_in, width_local), bf16),), [], 2 * US, 0,
        target, arrived.reshape(slots_in, width_local),
    )
    return (block_out, input_grad, mod_grad)


def solution(mesh):
    cut = Mesh(mesh.devices.reshape(SIZES), AXES)
    return jax.shard_map(
        body,
        mesh=cut,
        in_specs=(
            P(DP, TP),
            P(),
            P(),
            P(DP, TP),
            P(TP, DP),
            P(None, None, TP),
            P(DP, TP),
        ),
        out_specs=(P(DP, TP), P(DP, TP), P(None, None, TP)),
        check_vma=False,
    )
```

```python
import functools

import jax
import jax.numpy as jnp
from jax import lax
from jax.experimental import pallas as pl
from jax.experimental.pallas import tpu as pltpu
from jax.sharding import Mesh, PartitionSpec as P

GELU_K = 0.7978845608028654
GELU_C = 0.044715
EPS = 1e-06
AXES = ("zh", "y", "c", "zl", "x")
SIZES = (4, 4, 2, 4, 4)
DP = ("zh", "y", "c")
TP = ("zl", "x")
SAMPLES = 4
VMEM = 48 * 1024 * 1024
US = 10**9


def gelu_value(pre):
    inner = GELU_K * (pre + GELU_C * pre * pre * pre)
    return 0.5 * pre * (1.0 + jnp.tanh(inner))


def gelu_slope(pre):
    inner = GELU_K * (pre + GELU_C * pre * pre * pre)
    tangent = jnp.tanh(inner)
    return 0.5 * (1.0 + tangent) + 0.5 * pre * (1.0 - tangent * tangent) * GELU_K * (
        1.0 + 3.0 * GELU_C * pre * pre
    )


def shifted(value, axis, step):
    size = lax.axis_size(axis)
    return lax.ppermute(value, axis, [(i, (i + step) % size) for i in range(size)])


def crossed(value, axis, mask):
    size = lax.axis_size(axis)
    return lax.ppermute(value, axis, [(i, i ^ mask) for i in range(size)])


def direct_pieces(value, axis):
    return jnp.stack([value] + [shifted(value, axis, k) for k in (1, 2, 3)])


def spread(value, axis):
    copies = jnp.broadcast_to(value[None], (lax.axis_size(axis),) + value.shape)
    return lax.all_to_all(copies, axis, split_axis=0, concat_axis=0, tiled=True)


def summed(value, axis):
    mask = 1
    while mask < lax.axis_size(axis):
        value = value + crossed(value, axis, mask)
        mask *= 2
    return value


def three_terms(value):
    terms = []
    for _ in range(3):
        term = lax.reduce_precision(value, 8, 7)
        terms.append(term.astype(jnp.bfloat16))
        value = value - term
    return terms


def sample_mix(member, table):
    out = jnp.broadcast_to(table[SAMPLES - 1 : SAMPLES], (member.shape[0], table.shape[1]))
    for q in range(SAMPLES - 1):
        out = jnp.where(member[:, q : q + 1] > 0.5, table[q : q + 1], out)
    return out


def halves(c, half):
    first = pl.ds(pl.multiple_of(c * half, half), half)
    second = pl.ds(pl.multiple_of((1 - c) * half, half), half)
    return first, second


def zh_of(zh, n, count):
    step = jnp.where(n == 1, count - 1, jnp.where(n == 2, 1, jnp.where(n == 3, 2, 0)))
    return lax.rem(zh + step, count)


def weight_of(parts, n, which):
    group, place = ((0, 0), (1, 0), (1, 1), (2, 0))[n]
    return jnp.concatenate(
        [parts[group][0, place, which], parts[3 + group][0, place, which]], axis=0
    )


def gate_kernel(place, gathered, member, grad_out, table_out):
    y, zh, c = place[0], place[1], place[2]
    live = member[...]
    count = grad_out.shape[0]
    rows = grad_out.shape[2]
    half = grad_out.shape[3] // 2

    def step(index, carry):
        dy, n = index // count, index % count
        xi = lax.rem(y - dy + count, count)
        zi = zh_of(zh, n, count)
        block = zi * count + xi
        terms = gathered[block, rows : rows + 48].astype(jnp.float32)
        table = (terms[0:16] + terms[16:32]) + terms[32:48]
        table_out[block] = table
        grad = gathered[block, 0:rows].astype(jnp.float32)
        gated = (sample_mix(live, table[8:12]) * grad).astype(jnp.bfloat16)
        first, second = halves(c, half)
        grad_out[dy, n, :, first] = gated[:, :half]
        grad_out[dy, n, :, second] = gated[:, half:]
        return carry

    lax.fori_loop(0, count * count, step, 0)


def rows_kernel(place, rows, table_in, member, mod_out, average, inv_scale):
    y, zh, c = place[0], place[1], place[2]
    live = member[...]
    count = rows.shape[0]
    balanced = rows.shape[2]
    width = rows.shape[3]
    half = width // 2
    features = count * count * width

    total = jnp.zeros(rows.shape[2:], jnp.float32)
    for i in range(count):
        for j in range(count):
            total = total + rows[i, j].astype(jnp.float32)
    mean = jnp.sum(total, axis=1, keepdims=True) / features
    total = jnp.zeros(rows.shape[2:], jnp.float32)
    for i in range(count):
        for j in range(count):
            centred = rows[i, j].astype(jnp.float32) - mean
            total = total + centred * centred
    inv = lax.rsqrt(jnp.sum(total, axis=1, keepdims=True) / features + EPS)
    average[...] = mean
    inv_scale[...] = inv

    def step(index, carry):
        dy, n = index // count, index % count
        xi = lax.rem(y - dy + count, count)
        zi = zh_of(zh, n, count)
        table = table_in[zi * count + xi]
        shift, scale = table[0:4], 1.0 + table[4:8]
        normed = (rows[xi, zi].astype(jnp.float32) - mean) * inv
        value = (normed * sample_mix(live, scale) + sample_mix(live, shift)).astype(jnp.bfloat16)
        scale_hi = scale.astype(jnp.bfloat16).astype(jnp.float32)
        shift_hi = shift.astype(jnp.bfloat16).astype(jnp.float32)
        extra = jnp.concatenate(
            [scale_hi, scale - scale_hi, shift_hi, shift - shift_hi], axis=0
        ).astype(jnp.bfloat16)
        first, second = halves(c, half)
        mod_out[dy, n, 0:balanced, first] = value[:, :half]
        mod_out[dy, n, 0:balanced, second] = value[:, half:]
        mod_out[dy, n, balanced : balanced + 16, first] = extra[:, :half]
        mod_out[dy, n, balanced : balanced + 16, second] = extra[:, half:]
        return carry

    lax.fori_loop(0, count * count, step, 0)


def hidden_kernel(
    modulated, scaled, member, part0, part1, part2, part3, part4, part5,
    hidden_out, pre_grad_out, sums_out, pre_total, grad_total,
):
    parts = (part0, part1, part2, part3, part4, part5)
    live = member[...]
    rows = scaled.shape[2]
    step = pl.program_id(0)

    @pl.when(step == 0)
    def _():
        pre_total[...] = jnp.zeros_like(pre_total)
        grad_total[...] = jnp.zeros_like(grad_total)

    for n in range(scaled.shape[1]):
        up = weight_of(parts, n, 0)
        pre_total[...] += jnp.dot(modulated[0, n], up, preferred_element_type=jnp.float32)
        down = weight_of(parts, n, 1)
        grad_total[...] += jnp.dot(scaled[0, n], down, preferred_element_type=jnp.float32)

    @pl.when(step == pl.num_programs(0) - 1)
    def _():
        pre = pre_total[0:rows]
        extra = pre_total[rows : rows + 16]
        hidden_out[...] = gelu_value(pre).astype(jnp.bfloat16).T
        pre_grad = (grad_total[...] * gelu_slope(pre)).astype(jnp.bfloat16)
        pre_grad_out[...] = pre_grad.T
        pre_grad = pre_grad.astype(jnp.float32)
        scale_part = sample_mix(live, extra[0:4] + extra[4:8])
        shift_part = sample_mix(live, extra[8:12] + extra[12:16])
        first = jnp.sum(pre_grad * scale_part, axis=1, keepdims=True)
        second = jnp.sum(pre_grad * (pre - shift_part), axis=1, keepdims=True)
        lane = lax.broadcasted_iota(jnp.int32, (rows, 128), 1)
        both = jnp.where(lane == 0, first, jnp.where(lane == 1, second, 0.0))
        sums = both.T[0:8]
        high = sums.astype(jnp.bfloat16).astype(jnp.float32)
        sums_out[...] = jnp.concatenate([high, sums - high], axis=0).astype(jnp.bfloat16)


def outward_kernel(place, hidden, *refs):
    out = refs[-1]
    zh, c = place[1], place[2]
    count = out.shape[1]
    rows = out.shape[3]
    half = rows // 2
    low, high = halves(c, half)
    for n in range(count):
        weight = weight_of(refs[:6], n, 0)
        value = jnp.dot(weight, hidden[...], preferred_element_type=jnp.float32).astype(
            jnp.bfloat16
        )
        zi = zh_of(zh, n, count)
        out[0, zi, low, :] = value[:half]
        out[0, zi, high, :] = value[half:]
        if len(refs) == 8:
            out[0, zi, rows : rows + 16, :] = refs[6][...]


def joined_sums(terms):
    total = terms[0:8] + terms[8:16]
    high = total.astype(jnp.bfloat16).astype(jnp.float32)
    return jnp.concatenate([high, total - high], axis=0)


def fold_kernel(place, blocks, out):
    count, places, height, width = blocks.shape

    def step(m, carry):
        total = blocks[0, m].astype(jnp.float32)
        for k in range(1, count):
            total = total + blocks[k, m].astype(jnp.float32)
        out[m, 0:width] = total[0:width].astype(jnp.bfloat16)
        out[m, width:height] = joined_sums(total[width:height]).astype(jnp.bfloat16)
        return carry

    lax.fori_loop(0, places, step, 0)


def fold_out_kernel(place, blocks, grad, member, out):
    zl = place[3]
    count, places, width, _ = blocks.shape

    def step(m, carry):
        total = blocks[0, m].astype(jnp.float32)
        for k in range(1, count):
            total = total + blocks[k, m].astype(jnp.float32)
        to = lax.rem(m - zl + places, places)
        out[to, 0:width] = total.astype(jnp.bfloat16)
        part = image_sums(member[...], grad[m].astype(jnp.float32) * total.T)
        part = jnp.concatenate(part, axis=0)
        high = part.astype(jnp.bfloat16).astype(jnp.float32)
        middle = (part - high).astype(jnp.bfloat16).astype(jnp.float32)
        low = (part - high) - middle
        terms = jnp.concatenate([high, middle, low, jnp.zeros_like(low)], axis=0)
        out[to, width : width + 16] = terms.astype(jnp.bfloat16)
        return carry

    lax.fori_loop(0, places, step, 0)


def picked(index, values):
    lanes = lax.broadcasted_iota(jnp.int32, (index.shape[0], values.shape[0]), 1)
    chosen = jnp.where(lanes == index, 1.0, 0.0).astype(jnp.bfloat16)
    return jnp.dot(chosen, values, preferred_element_type=jnp.float32).astype(jnp.bfloat16)


def image_sums(live, values):
    return [
        jnp.sum(jnp.where(live[:, q : q + 1] > 0.5, values, 0.0), axis=0, keepdims=True)
        for q in range(SAMPLES)
    ]


def finish_in_kernel(
    features, pieces, rows, grad, average, inv_scale, member, table, index, back, totals
):
    live = member[...]
    balanced = rows.shape[0]
    total = pieces[0].astype(jnp.float32)
    for k in range(1, pieces.shape[0]):
        total = total + pieces[k].astype(jnp.float32)
    mod_in_grad = total[0:balanced].T
    sums = total[balanced : balanced + 8] + total[balanced + 8 : balanced + 16]
    means = jnp.concatenate([sums, jnp.zeros((120, balanced), jnp.float32)], axis=0).T / features
    inv = inv_scale[...]
    normed = (rows[...].astype(jnp.float32) - average[...]) * inv
    normed_grad = mod_in_grad * (1.0 + sample_mix(live, table[4:8]))
    row_grad = grad[...].astype(jnp.float32) + inv * (
        normed_grad - means[:, 0:1] - normed * means[:, 1:2]
    )
    back[...] = picked(index[...], row_grad.astype(jnp.bfloat16))
    totals[...] = jnp.concatenate(
        image_sums(live, mod_in_grad) + image_sums(live, mod_in_grad * normed), axis=0
    )


def finish_out_kernel(piece0, piece1, piece2, piece3, rows, member, table, out):
    live = member[...]
    balanced = rows.shape[0]
    branch = piece0[0:balanced].astype(jnp.float32)
    for piece in (piece1, piece2, piece3):
        branch = branch + piece[0:balanced].astype(jnp.float32)
    branch = branch.T
    gate = sample_mix(live, table[8:12])
    out[...] = (rows[...].astype(jnp.float32) + gate * branch).astype(jnp.bfloat16)


def send_kernel(position, live_rows, values, out):
    groups = live_rows.shape[0]
    slots = values.shape[0] // groups
    start = jnp.int32(0)
    for i in range(groups):
        start = start + jnp.where(i < position[0], live_rows[i], 0)
    row = lax.broadcasted_iota(jnp.int32, (values.shape[0], 1), 0)
    device = (row * (65536 // slots + 1)) >> 16
    index = ((device - start) & (groups - 1)) + groups * (row - slots * device)
    out[...] = picked(index, values[...])


def pick_kernel(index, values, out):
    out[...] = picked(index[...], values[...])


SMEM_SPEC = pl.BlockSpec(memory_space=pltpu.SMEM)
VMEM_SPEC = pl.BlockSpec(memory_space=pltpu.VMEM)


def call(kernel, outs, scratch, flops, moved, *args):
    return pl.pallas_call(
        kernel,
        out_shape=outs,
        in_specs=[SMEM_SPEC if a.ndim == 1 else VMEM_SPEC for a in args],
        out_specs=jax.tree.map(lambda _: VMEM_SPEC, outs),
        scratch_shapes=scratch,
        compiler_params=pltpu.CompilerParams(vmem_limit_bytes=VMEM),
        cost_estimate=pl.CostEstimate(flops=flops, bytes_accessed=moved, transcendentals=0),
    )(*args)


def body(hidden_in, live_rows, sample_tokens, w_up, w_down, modulation, out_grad):
    groups = lax.axis_size(DP)
    position = lax.axis_index(DP)
    slots_in = hidden_in.shape[0]
    per_pair = slots_in // groups
    balanced = out_grad.shape[0]
    width_local = hidden_in.shape[1]
    tensor_count = lax.axis_size(TP)
    model_width = width_local * tensor_count
    hid = w_up.shape[1]
    f32, bf16 = jnp.float32, jnp.bfloat16
    shape = jax.ShapeDtypeStruct
    low = groups - 1
    bits = groups.bit_length() - 1

    weights = jnp.stack([w_up, w_down.T])
    before = shifted(weights, "zh", 1)
    after = shifted(weights, "zh", -1)
    near = direct_pieces(weights[None], "y")

    table = modulation.reshape(-1, width_local)
    pad = jnp.zeros((16 - table.shape[0], width_local), f32)
    payload = jnp.concatenate([out_grad] + three_terms(jnp.concatenate([table, pad])), axis=0)

    row_ends = jnp.cumsum(live_rows)
    row_starts = row_ends - live_rows
    device_ids = jnp.arange(groups, dtype=jnp.int32)
    own_start = jnp.sum(jnp.where(device_ids < position, live_rows, 0))
    own_live = jnp.sum(jnp.where(device_ids == position, live_rows, 0))
    slot_ids = jnp.arange(per_pair, dtype=jnp.int32)[None, :]
    (outgoing,) = call(
        send_kernel, (shape((slots_in, width_local), bf16),), [], 2 * US, 0,
        position.astype(jnp.int32).reshape(1), live_rows, hidden_in,
    )
    outgoing = outgoing.reshape(groups, per_pair, width_local)
    gathered = lax.all_gather(payload, TP, axis=0)
    incoming = lax.all_to_all(outgoing, DP, split_axis=0, concat_axis=0, tiled=True)
    global_rows = position + groups * jnp.arange(balanced, dtype=jnp.int32)
    before_row = row_ends[None, :] <= global_rows[:, None]
    owners = jnp.sum(before_row.astype(jnp.int32), axis=1)
    owner_start = jnp.sum(jnp.where(before_row, live_rows[None, :], 0), axis=1)
    owner_slot = (global_rows - owner_start) >> bits
    incoming, before, after, near = lax.optimization_barrier((incoming, before, after, near))
    far = jnp.concatenate([shifted(before[:1], "zh", 1), shifted(after[1:], "zh", -1)], axis=0)
    pair = direct_pieces(jnp.stack([before, after]), "y")
    rows_bal = incoming.reshape(groups * per_pair, width_local)[owners * per_pair + owner_slot]
    sample_ends = jnp.cumsum(sample_tokens)
    sample_starts = sample_ends - sample_tokens
    member = (
        (global_rows[:, None] >= sample_starts[None, :])
        & (global_rows[:, None] < sample_ends[None, :])
    ).astype(f32)

    rows_zl = spread(rows_bal, "zl")
    rows_zl, far, pair = lax.optimization_barrier((rows_zl, far, pair))
    last = direct_pieces(far[None], "y")
    near_other = shifted(near, "c", 1)
    pair_other = shifted(pair, "c", 1)
    rows_all = spread(rows_zl, "x")

    by_place = gathered.reshape(4, 4, -1, width_local)
    grad_zl = lax.dynamic_index_in_dim(by_place, lax.axis_index("x"), 1, keepdims=False)
    grad_zl = grad_zl[:, :balanced]
    place = jnp.stack([lax.axis_index(a) for a in ("y", "zh", "c", "zl")]).astype(jnp.int32)
    block_shape = shape((4, 4, balanced, width_local), bf16)
    column = shape((balanced, 1), f32)
    scaled_grad, table_all = call(
        gate_kernel,
        (block_shape, shape((tensor_count, 16, width_local), f32)),
        [],
        4 * US,
        0,
        place, gathered, member,
    )
    rows_all, near_other, pair_other, last, scaled_grad = lax.optimization_barrier(
        (rows_all, near_other, pair_other, last, scaled_grad)
    )
    last_other = shifted(last, "c", 1)
    weight_parts = (near, pair, last, near_other, pair_other, last_other)
    modulated, average, inv_scale = call(
        rows_kernel,
        (shape((4, 4, balanced + 16, width_local), bf16), column, column),
        [],
        6 * US,
        0,
        place, rows_all, table_all, member,
    )
    unit_rows = shape((hid, balanced), bf16)
    whole = lambda *dims: pl.BlockSpec(dims, lambda *_: (0,) * len(dims))
    by_dy = lambda *dims: pl.BlockSpec((1,) + dims, lambda dy, *_: (dy,) + (0,) * len(dims))
    params = pltpu.CompilerParams(vmem_limit_bytes=VMEM)
    planes = weights.shape[1:]
    hidden, pre_grad, sums = pl.pallas_call(
        hidden_kernel,
        grid=(4,),
        out_shape=(unit_rows, unit_rows, shape((16, balanced), bf16)),
        in_specs=[
            by_dy(4, balanced + 16, width_local),
            by_dy(4, balanced, width_local),
            whole(balanced, SAMPLES),
        ]
        + [by_dy(n, 2, *planes) for n in (1, 2, 1)] * 2,
        out_specs=(whole(hid, balanced), whole(hid, balanced), whole(16, balanced)),
        scratch_shapes=[
            pltpu.VMEM((balanced + 16, hid), f32), pltpu.VMEM((balanced, hid), f32)
        ],
        compiler_params=params,
        cost_estimate=pl.CostEstimate(flops=8 * US, bytes_accessed=0, transcendentals=0),
    )(modulated, scaled_grad, member, *weight_parts)

    def outward(which, units, *extra):
        pick = lambda n: pl.BlockSpec(
            (1, n, 1) + planes, lambda dy, _: (dy, 0, which, 0, 0)
        )
        height = width_local + sum(e.shape[0] for e in extra)
        return pl.pallas_call(
            outward_kernel,
            grid_spec=pltpu.PrefetchScalarGridSpec(
                num_scalar_prefetch=1,
                grid=(4,),
                in_specs=[whole(hid, balanced)]
                + [pick(n) for n in (1, 2, 1)] * 2
                + [whole(*e.shape) for e in extra],
                out_specs=pl.BlockSpec(
                    (1, 4, height, balanced),
                    lambda dy, at: (lax.rem(at[0] - dy + 4, 4), 0, 0, 0),
                ),
            ),
            out_shape=shape((4, 4, height, balanced), bf16),
            compiler_params=params,
            cost_estimate=pl.CostEstimate(flops=5 * US, bytes_accessed=0, transcendentals=0),
        )(place, units, *weight_parts, *extra)

    partial_out = outward(1, hidden)
    partial_in = outward(0, pre_grad, sums)
    out_x = lax.all_to_all(partial_out, "x", split_axis=0, concat_axis=0, tiled=True)
    out_x, partial_in = lax.optimization_barrier((out_x, partial_in))
    in_x = lax.all_to_all(partial_in, "x", split_axis=0, concat_axis=0, tiled=True)
    (out_x,) = call(
        fold_out_kernel, (shape((4, width_local + 16, balanced), bf16),), [], 3 * US, 0,
        place, out_x, grad_zl, member,
    )
    out_zl = [out_x[0]] + [shifted(out_x[k], "zl", k) for k in (1, 2, 3)]
    in_x, out_zl = lax.optimization_barrier((in_x, out_zl))
    terms = jnp.sum(jnp.stack([o[width_local : width_local + 12] for o in out_zl]).astype(f32), 0)
    totals_out = (terms[0:4] + terms[4:8]) + terms[8:12]
    (in_x,) = call(fold_kernel, (shape(partial_in.shape[1:], bf16),), [], 2 * US, 0, place, in_x)
    in_zl = lax.all_to_all(in_x, "zl", split_axis=0, concat_axis=0, tiled=True)

    source_rows = ((position - row_starts[:, None]) & low) + groups * slot_ids
    back_index = jnp.where(
        source_rows < live_rows[:, None],
        (row_starts[:, None] + source_rows - position) >> bits,
        -1,
    ).reshape(-1, 1)
    returning, totals_in = call(
        functools.partial(finish_in_kernel, model_width),
        (shape((slots_in, width_local), bf16), shape((2 * SAMPLES, width_local), f32)),
        [], 4 * US, 0,
        in_zl, rows_bal, out_grad, average, inv_scale, member, table, back_index,
    )
    returning = returning.reshape(groups, per_pair, width_local)
    arrived = lax.all_to_all(returning, DP, split_axis=0, concat_axis=0, tiled=True)

    mod_grad = jnp.concatenate([totals_in, totals_out], axis=0)
    mod_grad = summed(summed(summed(mod_grad, "c"), "y"), "zh").reshape(modulation.shape)
    (block_out,) = call(
        finish_out_kernel, (shape((balanced, width_local), bf16),), [], 2 * US, 0,
        *out_zl, rows_bal, member, table,
    )

    own_rows = jnp.arange(slots_in, dtype=jnp.int32)
    target = ((own_start + own_rows) & low) * per_pair + (own_rows >> bits)
    target = jnp.where(own_rows < own_live, target, -1).reshape(-1, 1)
    (input_grad,) = call(
        pick_kernel, (shape((slots_in, width_local), bf16),), [], 2 * US, 0,
        target, arrived.reshape(slots_in, width_local),
    )
    return (block_out, input_grad, mod_grad)


def solution(mesh):
    cut = Mesh(mesh.devices.reshape(SIZES), AXES)
    return jax.shard_map(
        body,
        mesh=cut,
        in_specs=(
            P(DP, TP),
            P(),
            P(),
            P(DP, TP),
            P(TP, DP),
            P(None, None, TP),
            P(DP, TP),
        ),
        out_specs=(P(DP, TP), P(DP, TP), P(None, None, TP)),
        check_vma=False,
    )
```
